32 devices in a mesh: gx: 16 (over z, y, core), gy: 2 (over x).
Axes of the slice: x: 2, y: 2, z: 4, core: 2. Of those that a mesh axis runs over, the one named last changes fastest.
Arguments:
- hamiltonian: bfloat16 [32, 4, 8, 128, 128], P('gx', 'gy'), may hold values from -0.078125 to 0.078125
- neighbours: int32 [32, 4, 8], P('gx', 'gy'), may hold values from 0 to 8, as said below
- probe_seeds: int32 [256], replicated, may hold values from 0 to 1073741823
- coefficients: float32 [5], replicated, may hold values from 0.3 to 1
- cotangent: bfloat16 [32, 4, 128, 256], P('gx', 'gy'), may hold values from -6 to 6
Outputs:
- density: float32 [32, 4, 128, 256], P('gx', 'gy')
- grad_hamiltonian: bfloat16 [32, 4, 8, 128, 128], P('gx', 'gy')
The draws below stay inside these ranges and needn't reach their ends.
Inputs may be any that keep to these rules, and one draw needn't show every extreme that they name: `neighbours`: each block's list holds 8 different codes.
All inputs are finite; a program needn't handle non-finite values.
Results may differ from the reference program's by a relative error of at most 0.0064.
Values may be sent and summed in bfloat16 or wider, within the bound.
No kernel may reach another device: no remote copies, remote signals or barrier semaphores. Data moves between devices by JAX's collectives and lax.ppermute only.
A program may use at most 64 MiB of HBM per device.

```python
import jax
import jax.numpy as jnp

B = 128
P_SIZE = 256
K = 8
TERMS = 5
GBX = 32
GBY = 4


def draw_neighbours(key, part):
    missing = jax.random.randint(key, (GBX, GBY, 1), 0, 9, dtype=jnp.int32)
    slot_index = jnp.arange(K, dtype=jnp.int32)
    return slot_index + (slot_index >= missing).astype(jnp.int32)


def place_ends(entries, own_key, least, top_value):
    dims = entries.shape
    place = [jax.random.randint(jax.random.fold_in(own_key, axis), (), 0, dims[axis]) for axis in range(len(dims))]
    entries = entries.at[tuple(place)].set(least)
    longest = dims.index(max(dims))
    place[longest] = (place[longest] + 1) % dims[longest]
    return entries.at[tuple(place)].set(top_value)


def block_levels(rng, shape, split, smallest, top_value):
    def one(dim, blocks):
        draws = jax.random.uniform(jax.random.fold_in(jax.random.fold_in(rng, 6), dim), (blocks,), jnp.float32, smallest / len(split), top_value / len(split))
        return jnp.repeat(jnp.exp(draws), shape[dim] // blocks).reshape((-1,) + (1,) * (len(shape) - dim - 1))

    level = one(*split[0])
    for cut in split[1:]:
        level = level * one(*cut)
    return level


def gaussian(rng, dims, spread, most, pieces=(), kind=jnp.bfloat16):
    gain = block_levels(rng, dims, pieces, -0.22, 0.18) if pieces else 1.0
    drawn = jax.random.normal(rng, dims, jnp.float32) * spread * gain
    return jnp.minimum(jnp.maximum(drawn, -most), most).astype(kind)


def setup_inputs(seed: int = 0) -> dict:
    key_of = jax.random.split(jax.random.key(seed), 6)
    return {
        "hamiltonian": gaussian(key_of[0], (GBX, GBY, K, B, B), (25 * K * B // 4) ** -0.5, 0.078125, ((0, 16), (1, 2))),
        "neighbours": draw_neighbours(jax.random.fold_in(key_of[5], 71), 0),
        "probe_seeds": place_ends(jax.random.randint(key_of[2], (P_SIZE,), 0, 1073741824), jax.random.fold_in(key_of[2], 1), 0, 1073741823).astype(jnp.int32),
        "coefficients": jnp.clip(jax.random.uniform(key_of[3], (TERMS,), jnp.float32, 0.3, 1.0), 0.3, 1.0),
        "cotangent": gaussian(key_of[4], (GBX, GBY, B, P_SIZE), 1.0, 6.0, ((0, 16), (1, 2))),
    }


offset_table = tuple((offset_code // 3 - 1, offset_code % 3 - 1) for offset_code in range(9))


def probe_signs(global_rows, seed_values):
    hashed = global_rows[..., None] * jnp.int32(-1640531535)
    hashed = hashed ^ seed_values
    hashed = hashed ^ (hashed >> 15)
    hashed = hashed * jnp.int32(739982445)
    hashed = hashed ^ (hashed >> 12)
    parity = (hashed >> 7) & 1
    return (1 - 2 * parity).astype(jnp.float32)


def select_blocks(hamiltonian, neighbours, offset_code):
    chosen = jnp.zeros(hamiltonian.shape[:2] + hamiltonian.shape[3:], jnp.float32)
    for column in range(hamiltonian.shape[2]):
        chosen = chosen + jnp.where((neighbours[:, :, column] == offset_code)[:, :, None, None],
                                    hamiltonian[:, :, column].astype(jnp.float32), 0.0)
    return chosen.astype(jnp.bfloat16)


def forward_apply(selected, field_bf16):
    summed = jnp.zeros(field_bf16.shape, jnp.float32)
    for offset_code, (step_x, step_y) in enumerate(offset_table):
        moved = jnp.roll(field_bf16, (-step_x, -step_y), (0, 1)).astype(jnp.float32)
        summed = summed + jnp.einsum('abxy,abyp->abxp', selected[offset_code].astype(jnp.float32), moved)
    return summed


def transpose_apply(selected, field_bf16):
    summed = jnp.zeros(field_bf16.shape, jnp.float32)
    for offset_code, (step_x, step_y) in enumerate(offset_table):
        product = jnp.einsum('abyx,abyp->abxp', selected[offset_code].astype(jnp.float32), field_bf16.astype(jnp.float32))
        summed = summed + jnp.roll(product, (step_x, step_y), (0, 1))
    return summed


def reference(hamiltonian, neighbours, probe_seeds, coefficients, cotangent):
    place_x = jnp.arange(GBX, dtype=jnp.int32)
    place_y = jnp.arange(GBY, dtype=jnp.int32)
    orbital = jnp.arange(B, dtype=jnp.int32)
    global_rows = (place_x[:, None] * GBY + place_y[None, :])[:, :, None] * B + orbital[None, None, :]
    start_term = probe_signs(global_rows, probe_seeds)
    selected = [select_blocks(hamiltonian, neighbours, offset_code) for offset_code in range(9)]
    rounded_terms = [start_term.astype(jnp.bfloat16)]
    previous = start_term
    current = forward_apply(selected, rounded_terms[0])
    density = coefficients[0] * start_term + coefficients[1] * current
    for index in range(2, TERMS):
        rounded_terms.append(current.astype(jnp.bfloat16))
        following = 2.0 * forward_apply(selected, rounded_terms[-1]) - previous
        previous, current = current, following
        density = density + coefficients[index] * current
    seed_field = cotangent.astype(jnp.float32)
    adjoints = {}
    adjoint_rounded = {}
    for index in range(TERMS - 1, 0, -1):
        value = coefficients[index] * seed_field
        if index + 1 < TERMS:
            value = value + 2.0 * transpose_apply(selected, adjoint_rounded[index + 1])
        if index + 2 < TERMS:
            value = value - adjoints[index + 2]
        adjoints[index] = value
        adjoint_rounded[index] = value.astype(jnp.bfloat16)
    gradient = jnp.zeros(hamiltonian.shape, jnp.float32)
    for offset_code, (step_x, step_y) in enumerate(offset_table):
        block_grad = jnp.zeros((GBX, GBY, B, B), jnp.float32)
        for index in range(1, TERMS):
            factor = 1.0 if index == 1 else 2.0
            moved = jnp.roll(rounded_terms[index - 1], (-step_x, -step_y), (0, 1)).astype(jnp.float32)
            weighted = (adjoint_rounded[index] * factor).astype(jnp.float32)
            block_grad = block_grad + jnp.einsum('abxp,abyp->abxy', weighted, moved)
        gradient = gradient + jnp.where((neighbours == offset_code)[..., None, None], block_grad[:, :, None], 0.0)
    return density, (gradient * (1.0 / P_SIZE)).astype(jnp.bfloat16)
```

```python
import functools

import jax
import jax.numpy as jnp
from jax import lax
from jax.experimental import pallas as pl
from jax.experimental.pallas import tpu as pltpu
from jax.sharding import PartitionSpec as P

offset_table = tuple(((offset_code // 3 - 1, offset_code % 3 - 1) for offset_code in range(9)))


def shifted(value, axis, steps):
    count = lax.axis_size(axis)
    pairs = [(source, (source + steps) % count) for source in range(count)]
    return lax.ppermute(value, axis, pairs)


def padded_2(block, sides, width):
    for axis, dim in sides:
        count = lax.axis_size(axis)
        forward = [(i, i + 1) for i in range(count - 1)]
        forward.append((count - 1, 0))
        backward = [(target, source) for source, target in forward]
        low = lax.ppermute(
            lax.slice_in_dim(block, block.shape[dim] - width, None, axis=dim), axis, forward
        )
        high = lax.ppermute(lax.slice_in_dim(block, 0, width, axis=dim), axis, backward)
        block = jnp.concatenate([low, block, high], axis=dim)
    return block


def probe_signs(global_rows, seed_values):
    hashed = global_rows[..., None] * jnp.int32(-1640531535)
    hashed = hashed ^ seed_values
    hashed = hashed ^ hashed >> 15
    hashed = hashed * jnp.int32(739982445)
    hashed = hashed ^ hashed >> 12
    parity = hashed >> 7 & 1
    return (1 - 2 * parity).astype(jnp.float32)


def by_offset(hamiltonian, neighbours):
    onehot = (neighbours[..., None] == jnp.arange(9, dtype=jnp.int32)).astype(jnp.bfloat16)
    picked = jnp.einsum(
        "abkc,abkxy->abcxy", onehot, hamiltonian, preferred_element_type=jnp.float32
    )
    return picked.astype(jnp.bfloat16)


def forward_apply(selected, padded):
    rows_x, rows_y = (selected.shape[0], selected.shape[1])
    summed = jnp.zeros((rows_x, rows_y, selected.shape[3], padded.shape[3]), jnp.float32)
    for offset_code, (step_x, step_y) in enumerate(offset_table):
        window = padded[1 + step_x : 1 + step_x + rows_x, 1 + step_y : 1 + step_y + rows_y]
        summed = summed + jnp.einsum(
            "abxy,abyp->abxp",
            selected[:, :, offset_code],
            window,
            preferred_element_type=jnp.float32,
        )
    return summed


def push_transpose(selected, adjoint_bf16):
    rows_x, rows_y = (selected.shape[0], selected.shape[1])
    gathered = jnp.zeros((rows_x + 2, rows_y + 2) + adjoint_bf16.shape[2:], jnp.float32)
    for offset_code, (step_x, step_y) in enumerate(offset_table):
        product = jnp.einsum(
            "abyx,abyp->abxp",
            selected[:, :, offset_code],
            adjoint_bf16,
            preferred_element_type=jnp.float32,
        )
        gathered = gathered + jnp.pad(
            product, ((1 + step_x, 1 - step_x), (1 + step_y, 1 - step_y), (0, 0), (0, 0))
        )
    for offset_by, source, target in ((-1, 0, rows_x), (1, rows_x + 1, 1)):
        moved = shifted(gathered[source], "gx", offset_by)
        gathered = gathered.at[target].add(moved)
    middle = gathered[1 : rows_x + 1]
    for offset_by, source, target in ((-1, 0, rows_y), (1, rows_y + 1, 1)):
        moved = shifted(middle[:, source], "gy", offset_by)
        middle = middle.at[:, target].add(moved)
    return middle[:, 1 : rows_y + 1]


def any_shards(hamiltonian, neighbours, probe_seeds, coefficients, cotangent):
    rows_x, rows_y = (hamiltonian.shape[0], hamiltonian.shape[1])
    width = hamiltonian.shape[3]
    probes = cotangent.shape[3]
    count_terms = coefficients.shape[0]
    span_x = rows_x * lax.axis_size("gx")
    span_y = rows_y * lax.axis_size("gy")
    place_x = (lax.axis_index("gx") * rows_x + jnp.arange(rows_x + 2, dtype=jnp.int32) - 1) % span_x
    place_y = (lax.axis_index("gy") * rows_y + jnp.arange(rows_y + 2, dtype=jnp.int32) - 1) % span_y
    orbital = jnp.arange(width, dtype=jnp.int32)
    global_rows = (place_x[:, None] * span_y + place_y[None, :])[:, :, None] * width + orbital[
        None, None, :
    ]
    start_padded = probe_signs(global_rows, probe_seeds)
    start_term = start_padded[1 : rows_x + 1, 1 : rows_y + 1]
    selected = by_offset(hamiltonian, neighbours)
    term_pads = [start_padded.astype(jnp.bfloat16)]
    previous = start_term
    current = forward_apply(selected, term_pads[0])
    density = coefficients[0] * start_term + coefficients[1] * current
    for index in range(2, count_terms):
        padded = padded_2(current.astype(jnp.bfloat16), (("gx", 0), ("gy", 1)), 1)
        term_pads.append(padded)
        following = 2.0 * forward_apply(selected, padded) - previous
        previous, current = (current, following)
        density = density + coefficients[index] * current
    seed_field = cotangent.astype(jnp.float32)
    adjoints = {}
    adjoint_rounded = {}
    for index in range(count_terms - 1, 0, -1):
        value = coefficients[index] * seed_field
        if index + 1 < count_terms:
            carried = push_transpose(selected, adjoint_rounded[index + 1])
            value = value + 2.0 * carried
        if index + 2 < count_terms:
            value = value - adjoints[index + 2]
        adjoints[index] = value
        adjoint_rounded[index] = value.astype(jnp.bfloat16)
    adjoint_stack = jnp.concatenate(
        [adjoint_rounded[index] * (1.0 if index == 1 else 2.0) for index in range(1, count_terms)],
        axis=3,
    )
    term_stack = jnp.concatenate(term_pads, axis=3)
    gradient = jnp.zeros(hamiltonian.shape, jnp.float32)
    for offset_code, (step_x, step_y) in enumerate(offset_table):
        window = term_stack[1 + step_x : 1 + step_x + rows_x, 1 + step_y : 1 + step_y + rows_y]
        block_grad = jnp.einsum(
            "abxq,abyq->abxy", adjoint_stack, window, preferred_element_type=jnp.float32
        )
        gradient = gradient + jnp.where(
            (neighbours == offset_code)[..., None, None], block_grad[:, :, None], 0.0
        )
    return (density, (gradient * (1.0 / probes)).astype(jnp.bfloat16))


bf16 = jnp.bfloat16
f32 = jnp.float32
VMEM_BYTES = 48 * 1024 * 1024


def swap_y(value):
    return lax.ppermute(value, "gy", [(0, 1), (1, 0)])


def swap_near(value):
    count = lax.axis_size("gx")
    return lax.ppermute(value, "gx", [(i, i ^ 1) for i in range(count)])


def swap_far(value):
    count = lax.axis_size("gx")
    pairs = [(i, (i + 1) % count if i % 2 else (i - 1) % count) for i in range(count)]
    return lax.ppermute(value, "gx", pairs)


def load_window(parts, window, sems):
    copies = [
        pltpu.make_async_copy(part, window.at[pl.ds(4 * at, 4)], sems.at[at])
        for at, part in enumerate(parts)
    ]
    for copy in copies:
        copy.start()
    for copy in copies:
        copy.wait()


def window_product(slots, step, h_ref, window, listed):
    total = None
    for k in range(0, listed, 2):
        left = jnp.concatenate([h_ref[0, 0, k], h_ref[0, 0, k + 1]], axis=1)
        right = jnp.concatenate(
            [window[slots[step * listed + k]], window[slots[step * listed + k + 1]]], axis=0
        )
        part = jnp.dot(left, right, preferred_element_type=f32)
        total = part if total is None else total + part
    return total


def first_forward_kernel(listed, rows, slots, h_ref, w_ref, term_ref, rounded_ref):
    value = window_product(slots, pl.program_id(0), h_ref, w_ref, listed)
    term_ref[0] = value
    rounded_ref[0] = value.astype(bf16)


def next_forward_kernel(
    index, last, listed, rows, slots, coef, h_ref, far, outer, inner, near, before_ref, *rest
):
    refs = list(rest)
    sums_ref = refs.pop(0)
    if index == 2:
        sums_ref, first_ref = None, sums_ref
    if last:
        density_ref, window, sems = refs
    else:
        term_ref, rounded_ref, density_ref, window, sems = refs
    step = pl.program_id(0)

    @pl.when(step == 0)
    def _():
        load_window((far, outer, inner, near), window, sems)

    before = before_ref[0].astype(f32)
    value = 2.0 * window_product(slots, step, h_ref, window, listed) - before
    if index == 2:
        sums = coef[0] * before + coef[1] * first_ref[0]
    else:
        sums = sums_ref[0]
    sums = sums + coef[index] * value
    if last:
        density_ref[0, 0] = sums
    else:
        term_ref[0] = value
        rounded_ref[0] = value.astype(bf16)
        density_ref[0] = sums


def push(slots, step, h_ref, adjoint_t, sums, listed):
    wide = jnp.concatenate([h_ref[0, 0, k] for k in range(listed)], axis=1)
    product = jnp.dot(adjoint_t, wide, preferred_element_type=f32)
    width = wide.shape[0]
    for k in range(listed):
        slot = slots[step * listed + k]
        sums[slot] += product[:, k * width : (k + 1) * width]


def finish_push(far_ref, near_ref, middle_ref, sums):
    far_ref[...] = sums[0:4].astype(bf16)
    near_ref[...] = sums[12:16].astype(bf16)
    middle_ref[...] = sums[4:12]


def first_adjoint_kernel(
    top, listed, rows, slots, coef, h_ref, cot_ref, cot_t_ref, value_ref, rounded_ref, far_ref, near_ref, middle_ref, sums
):
    step = pl.program_id(0)

    @pl.when(step == 0)
    def _():
        sums[...] = jnp.zeros_like(sums)

    cot = cot_ref[0, 0].astype(f32)
    rounded_ref[0] = (coef[top] * cot).astype(bf16)
    cot_t = jnp.transpose(cot)
    cot_t_ref[0] = cot_t.astype(bf16)
    value = coef[top] * cot_t
    value_ref[0] = value
    push(slots, step, h_ref, value.astype(bf16), sums, listed)

    @pl.when(step == pl.num_programs(0) - 1)
    def _():
        finish_push(far_ref, near_ref, middle_ref, sums)


def adjoint_value(index, coef, cot_t_ref, own_ref, came_ref, across_ref):
    carried = own_ref[0] + came_ref[0].astype(f32) + across_ref[0].astype(f32)
    return coef[index] * cot_t_ref[0].astype(f32) + 2.0 * carried


def next_adjoint_kernel(
    index, listed, has_older, rows, slots, coef, h_ref, cot_t_ref, own_ref, came_ref, across_ref, *rest
):
    refs = list(rest)
    older_ref = refs.pop(0) if has_older else None
    value_ref, rounded_ref, far_ref, near_ref, middle_ref, sums = refs
    step = pl.program_id(0)

    @pl.when(step == 0)
    def _():
        sums[...] = jnp.zeros_like(sums)

    value = adjoint_value(index, coef, cot_t_ref, own_ref, came_ref, across_ref)
    if has_older:
        value = value - older_ref[0]
    value_ref[0] = value
    rounded_ref[0] = jnp.transpose(value).astype(bf16)
    push(slots, step, h_ref, value.astype(bf16), sums, listed)

    @pl.when(step == pl.num_programs(0) - 1)
    def _():
        finish_push(far_ref, near_ref, middle_ref, sums)


def gradient_kernel(
    terms, listed, scale, rows, slots, coef, cot_t_ref, own_ref, came_ref, across_ref, older_ref, *rest
):
    refs = list(rest)
    adjoints = refs[: terms - 2]
    start = refs[terms - 2]
    later = refs[terms - 1 : terms - 1 + 4 * (terms - 2)]
    grad_ref, window, sems = refs[terms - 1 + 4 * (terms - 2) :]
    step = pl.program_id(0)

    @pl.when(step == 0)
    def _():
        copies = [pltpu.make_async_copy(start, window.at[0], sems.at[0])]
        for t in range(terms - 2):
            for at in range(4):
                copies.append(
                    pltpu.make_async_copy(
                        later[4 * t + at], window.at[t + 1, pl.ds(4 * at, 4)], sems.at[1 + 4 * t + at]
                    )
                )
        for copy in copies:
            copy.start()
        for copy in copies:
            copy.wait()

    value = adjoint_value(1, coef, cot_t_ref, own_ref, came_ref, across_ref) - older_ref[0]
    first = jnp.transpose(value).astype(bf16)
    left = jnp.concatenate([first] + [a[0] * bf16(2.0) for a in adjoints], axis=1)
    for k in range(listed):
        slot = slots[step * listed + k]
        right = jnp.concatenate([window[t, slot] for t in range(terms - 1)], axis=1)
        total = lax.dot_general(left, right, (((1,), (1,)), ((), ())), preferred_element_type=f32)
        grad_ref[0, 0, k] = (total * scale).astype(bf16)


def pair_shards(hamiltonian, neighbours, probe_seeds, coefficients, cotangent):
    rows_x, rows_y, listed, width = hamiltonian.shape[:4]
    probes = cotangent.shape[3]
    terms = coefficients.shape[0]
    span_x = rows_x * lax.axis_size("gx")
    span_y = rows_y * lax.axis_size("gy")
    odd = lax.axis_index("gx") % 2
    sign = 1 - 2 * odd
    four = jnp.arange(4, dtype=jnp.int32)
    local_row = jnp.where(odd == 0, four - 1, 2 - four)
    place_x = (lax.axis_index("gx") * rows_x + local_row) % span_x
    place_y = (lax.axis_index("gy") * rows_y + four) % span_y
    orbital = jnp.arange(width, dtype=jnp.int32)
    global_rows = (place_x[:, None] * span_y + place_y).reshape(16)[:, None] * width + orbital
    start = probe_signs(global_rows, probe_seeds).astype(bf16)
    rows = jnp.stack([odd, 1 - odd]).astype(jnp.int32)
    codes = jnp.where(odd == 0, neighbours, neighbours[::-1])
    window_row = 1 + jnp.arange(2, dtype=jnp.int32)[:, None, None] + sign * (codes // 3 - 1)
    window_col = (jnp.arange(2, dtype=jnp.int32)[None, :, None] + codes % 3 - 1) % 4
    slots = (window_row * 4 + window_col).reshape(-1).astype(jnp.int32)

    blocks = rows_x * rows_y
    whole = lambda *shape: pl.BlockSpec(shape, lambda g, *_: (0,) * len(shape))
    h_spec = pl.BlockSpec(
        (1, 1, listed, width, width), lambda g, rows, *_: (rows[g // 2], g % 2, 0, 0, 0)
    )
    f_spec = pl.BlockSpec((1, width, probes), lambda g, *_: (g, 0, 0))
    t_spec = pl.BlockSpec((1, probes, width), lambda g, *_: (g, 0, 0))
    natural_spec = pl.BlockSpec((1, 1, width, probes), lambda g, rows, *_: (rows[g // 2], g % 2, 0, 0))
    any_spec = pl.BlockSpec(memory_space=pl.ANY)
    fields = jax.ShapeDtypeStruct((blocks, width, probes), bf16)
    fields_f32 = jax.ShapeDtypeStruct((blocks, width, probes), f32)
    turned = jax.ShapeDtypeStruct((blocks, probes, width), bf16)
    turned_f32 = jax.ShapeDtypeStruct((blocks, probes, width), f32)
    apply_flops = 2 * blocks * listed * width * width * probes

    def call(kernel, scalars, in_specs, operands, out_specs, out_shape, scratch, flops, name):
        return pl.pallas_call(
            kernel,
            grid_spec=pltpu.PrefetchScalarGridSpec(
                num_scalar_prefetch=len(scalars),
                grid=(blocks,),
                in_specs=in_specs,
                out_specs=out_specs,
                scratch_shapes=scratch,
            ),
            out_shape=out_shape,
            compiler_params=pltpu.CompilerParams(
                dimension_semantics=("arbitrary",), vmem_limit_bytes=VMEM_BYTES
            ),
            cost_estimate=pl.CostEstimate(
                flops=flops, bytes_accessed=4 * 1024 * 1024, transcendentals=0
            ),
            name=name,
        )(*scalars, *operands)

    window_scratch = [
        pltpu.VMEM((16, width, probes), bf16),
        pltpu.SemaphoreType.DMA((4,)),
    ]
    sums_scratch = [pltpu.VMEM((16, probes, width), f32)]

    term, rounded = call(
        functools.partial(first_forward_kernel, listed),
        (rows, slots), [h_spec, whole(16, width, probes)], (hamiltonian, start),
        [f_spec, f_spec], [fields_f32, fields], [], apply_flops, "forward_1",
    )
    push_specs = [whole(4, probes, width), whole(4, probes, width), whole(8, probes, width)]
    row_t = jax.ShapeDtypeStruct((4, probes, width), bf16)
    push_shapes = [row_t, row_t, jax.ShapeDtypeStruct((8, probes, width), f32)]
    top = terms - 1
    cot_t, value, adj_rounded, to_far, to_near, middle = call(
        functools.partial(first_adjoint_kernel, top, listed),
        (rows, slots, coefficients), [h_spec, natural_spec], (hamiltonian, cotangent),
        [t_spec, t_spec, f_spec] + push_specs, [turned, turned_f32, fields] + push_shapes,
        sums_scratch, apply_flops, "adjoint_top",
    )
    adjoints = {top: value}
    adjoints_rounded = {top: adj_rounded}
    values = {0: start[4:12].reshape(2, 4, width, probes)[:, :2].reshape(4, width, probes), 1: term}
    windows = []
    density = None
    for index in range(2, terms):
        across = swap_y(rounded)
        outer = jnp.concatenate([rounded[:2], across[:2]])
        inner = jnp.concatenate([rounded[2:], across[2:]])
        near = swap_near(inner)
        far = swap_far(outer)
        from_far = swap_far(to_far)
        from_near = swap_near(to_near)
        came = jnp.concatenate([from_far, from_near])
        total = middle + came.astype(f32)
        to_across = jnp.concatenate([total[2:4], total[6:8]]).astype(bf16)
        from_across = swap_y(to_across)
        own = jnp.concatenate([middle[:2], middle[4:6]])
        came_own = jnp.concatenate([came[:2], came[4:6]])

        windows.append((far, outer, inner, near))
        last = index == terms - 1
        sums = values[1] if index == 2 else density
        out = call(
            functools.partial(next_forward_kernel, index, last, listed),
            (rows, slots, coefficients),
            [h_spec] + [any_spec] * 4 + [f_spec, f_spec],
            (hamiltonian, far, outer, inner, near, values[index - 2], sums),
            [natural_spec] if last else [f_spec, f_spec, f_spec],
            [jax.ShapeDtypeStruct(cotangent.shape, f32)] if last else [fields_f32, fields, fields_f32],
            window_scratch, apply_flops, "forward_next",
        )
        if last:
            density = out[0]
        else:
            values[index], rounded, density = out
        at = terms - index
        if at > 1:
            has_older = at + 2 < terms
            out = call(
                functools.partial(next_adjoint_kernel, at, listed, has_older),
                (rows, slots, coefficients),
                [h_spec] + [t_spec] * (5 if has_older else 4),
                (hamiltonian, cot_t, own, came_own, from_across)
                + ((adjoints[at + 2],) if has_older else ()),
                [t_spec, f_spec] + push_specs, [turned_f32, fields] + push_shapes,
                sums_scratch, apply_flops, "adjoint_next",
            )
            adjoints[at], adjoints_rounded[at], to_far, to_near, middle = out
    (gradient,) = call(
        functools.partial(gradient_kernel, terms, listed, 1.0 / probes),
        (rows, slots, coefficients),
        [t_spec] * 5 + [f_spec] * (terms - 2) + [any_spec] * (1 + 4 * (terms - 2)),
        (cot_t, own, came_own, from_across, adjoints[3])
        + tuple(adjoints_rounded[t] for t in range(2, terms))
        + (start,) + tuple(part for window in windows for part in window),
        [h_spec], [jax.ShapeDtypeStruct(hamiltonian.shape, bf16)],
        [
            pltpu.VMEM((terms - 1, 16, width, probes), bf16),
            pltpu.SemaphoreType.DMA((1 + 4 * (terms - 2),)),
        ],
        (terms - 1) * apply_flops, "gradient",
    )
    return density, gradient


def shards(hamiltonian, neighbours, probe_seeds, coefficients, cotangent):
    paired = (
        hamiltonian.shape[:2] == (2, 2)
        and lax.axis_size("gy") == 2
        and lax.axis_size("gx") % 2 == 0
        and hamiltonian.shape[2] % 2 == 0
        and coefficients.shape[0] > 3
    )
    run = pair_shards if paired else any_shards
    return run(hamiltonian, neighbours, probe_seeds, coefficients, cotangent)


def solution(mesh):
    placed = (
        P("gx", "gy", None, None, None),
        P("gx", "gy", None),
        P(),
        P(),
        P("gx", "gy", None, None),
    )
    return jax.shard_map(
        shards,
        mesh=mesh,
        in_specs=placed,
        out_specs=(P("gx", "gy", None, None), P("gx", "gy", None, None, None)),
        check_vma=False,
    )
```

```python
import functools

import jax
import jax.numpy as jnp
from jax import lax
from jax.experimental import pallas as pl
from jax.experimental.pallas import tpu as pltpu
from jax.sharding import PartitionSpec as P

offset_table = tuple(((offset_code // 3 - 1, offset_code % 3 - 1) for offset_code in range(9)))


def shifted(value, axis, steps):
    count = lax.axis_size(axis)
    pairs = [(source, (source + steps) % count) for source in range(count)]
    return lax.ppermute(value, axis, pairs)


def padded_2(block, sides, width):
    for axis, dim in sides:
        count = lax.axis_size(axis)
        forward = [(i, i + 1) for i in range(count - 1)]
        forward.append((count - 1, 0))
        backward = [(target, source) for source, target in forward]
        low = lax.ppermute(
            lax.slice_in_dim(block, block.shape[dim] - width, None, axis=dim), axis, forward
        )
        high = lax.ppermute(lax.slice_in_dim(block, 0, width, axis=dim), axis, backward)
        block = jnp.concatenate([low, block, high], axis=dim)
    return block


def probe_signs(global_rows, seed_values):
    hashed = global_rows[..., None] * jnp.int32(-1640531535)
    hashed = hashed ^ seed_values
    hashed = hashed ^ hashed >> 15
    hashed = hashed * jnp.int32(739982445)
    hashed = hashed ^ hashed >> 12
    parity = hashed >> 7 & 1
    return (1 - 2 * parity).astype(jnp.float32)


def by_offset(hamiltonian, neighbours):
    onehot = (neighbours[..., None] == jnp.arange(9, dtype=jnp.int32)).astype(jnp.bfloat16)
    picked = jnp.einsum(
        "abkc,abkxy->abcxy", onehot, hamiltonian, preferred_element_type=jnp.float32
    )
    return picked.astype(jnp.bfloat16)


def forward_apply(selected, padded):
    rows_x, rows_y = (selected.shape[0], selected.shape[1])
    summed = jnp.zeros((rows_x, rows_y, selected.shape[3], padded.shape[3]), jnp.float32)
    for offset_code, (step_x, step_y) in enumerate(offset_table):
        window = padded[1 + step_x : 1 + step_x + rows_x, 1 + step_y : 1 + step_y + rows_y]
        summed = summed + jnp.einsum(
            "abxy,abyp->abxp",
            selected[:, :, offset_code],
            window,
            preferred_element_type=jnp.float32,
        )
    return summed


def push_transpose(selected, adjoint_bf16):
    rows_x, rows_y = (selected.shape[0], selected.shape[1])
    gathered = jnp.zeros((rows_x + 2, rows_y + 2) + adjoint_bf16.shape[2:], jnp.float32)
    for offset_code, (step_x, step_y) in enumerate(offset_table):
        product = jnp.einsum(
            "abyx,abyp->abxp",
            selected[:, :, offset_code],
            adjoint_bf16,
            preferred_element_type=jnp.float32,
        )
        gathered = gathered + jnp.pad(
            product, ((1 + step_x, 1 - step_x), (1 + step_y, 1 - step_y), (0, 0), (0, 0))
        )
    for offset_by, source, target in ((-1, 0, rows_x), (1, rows_x + 1, 1)):
        moved = shifted(gathered[source], "gx", offset_by)
        gathered = gathered.at[target].add(moved)
    middle = gathered[1 : rows_x + 1]
    for offset_by, source, target in ((-1, 0, rows_y), (1, rows_y + 1, 1)):
        moved = shifted(middle[:, source], "gy", offset_by)
        middle = middle.at[:, target].add(moved)
    return middle[:, 1 : rows_y + 1]


def any_shards(hamiltonian, neighbours, probe_seeds, coefficients, cotangent):
    rows_x, rows_y = (hamiltonian.shape[0], hamiltonian.shape[1])
    width = hamiltonian.shape[3]
    probes = cotangent.shape[3]
    count_terms = coefficients.shape[0]
    span_x = rows_x * lax.axis_size("gx")
    span_y = rows_y * lax.axis_size("gy")
    place_x = (lax.axis_index("gx") * rows_x + jnp.arange(rows_x + 2, dtype=jnp.int32) - 1) % span_x
    place_y = (lax.axis_index("gy") * rows_y + jnp.arange(rows_y + 2, dtype=jnp.int32) - 1) % span_y
    orbital = jnp.arange(width, dtype=jnp.int32)
    global_rows = (place_x[:, None] * span_y + place_y[None, :])[:, :, None] * width + orbital[
        None, None, :
    ]
    start_padded = probe_signs(global_rows, probe_seeds)
    start_term = start_padded[1 : rows_x + 1, 1 : rows_y + 1]
    selected = by_offset(hamiltonian, neighbours)
    term_pads = [start_padded.astype(jnp.bfloat16)]
    previous = start_term
    current = forward_apply(selected, term_pads[0])
    density = coefficients[0] * start_term + coefficients[1] * current
    for index in range(2, count_terms):
        padded = padded_2(current.astype(jnp.bfloat16), (("gx", 0), ("gy", 1)), 1)
        term_pads.append(padded)
        following = 2.0 * forward_apply(selected, padded) - previous
        previous, current = (current, following)
        density = density + coefficients[index] * current
    seed_field = cotangent.astype(jnp.float32)
    adjoints = {}
    adjoint_rounded = {}
    for index in range(count_terms - 1, 0, -1):
        value = coefficients[index] * seed_field
        if index + 1 < count_terms:
            carried = push_transpose(selected, adjoint_rounded[index + 1])
            value = value + 2.0 * carried
        if index + 2 < count_terms:
            value = value - adjoints[index + 2]
        adjoints[index] = value
        adjoint_rounded[index] = value.astype(jnp.bfloat16)
    adjoint_stack = jnp.concatenate(
        [adjoint_rounded[index] * (1.0 if index == 1 else 2.0) for index in range(1, count_terms)],
        axis=3,
    )
    term_stack = jnp.concatenate(term_pads, axis=3)
    gradient = jnp.zeros(hamiltonian.shape, jnp.float32)
    for offset_code, (step_x, step_y) in enumerate(offset_table):
        window = term_stack[1 + step_x : 1 + step_x + rows_x, 1 + step_y : 1 + step_y + rows_y]
        block_grad = jnp.einsum(
            "abxq,abyq->abxy", adjoint_stack, window, preferred_element_type=jnp.float32
        )
        gradient = gradient + jnp.where(
            (neighbours == offset_code)[..., None, None], block_grad[:, :, None], 0.0
        )
    return (density, (gradient * (1.0 / probes)).astype(jnp.bfloat16))


bf16 = jnp.bfloat16
f32 = jnp.float32
VMEM_BYTES = 40 * 1024 * 1024
OWN = (4, 5, 8, 9)
ACROSS = (6, 7, 10, 11)


def swap_y(value):
    return lax.ppermute(value, "gy", [(0, 1), (1, 0)])


def swap_near(value):
    count = lax.axis_size("gx")
    return lax.ppermute(value, "gx", [(i, i ^ 1) for i in range(count)])


def swap_far(value):
    count = lax.axis_size("gx")
    pairs = [(i, (i + 1) % count if i % 2 else (i - 1) % count) for i in range(count)]
    return lax.ppermute(value, "gx", pairs)


def start_signs(rows_from, seeds, width):
    shape = (width, seeds.shape[1])
    hashed = (rows_from + lax.broadcasted_iota(jnp.int32, shape, 0)) * jnp.int32(-1640531535)
    hashed = hashed ^ seeds
    hashed = hashed ^ hashed >> 15
    hashed = hashed * jnp.int32(739982445)
    hashed = hashed ^ hashed >> 12
    return (1 - 2 * (hashed >> 7 & 1)).astype(f32).astype(bf16)


def listed_blocks(h_ref, rows, at):
    return [h_ref[rows[at // 2], at % 2, k] for k in range(h_ref.shape[2])]


def window_product(slots, rows, at, h_ref, window):
    listed = h_ref.shape[2]
    left = jnp.concatenate(listed_blocks(h_ref, rows, at), axis=1)
    right = jnp.concatenate([window[slots[at * listed + k]] for k in range(listed)], axis=0)
    return jnp.dot(left, right, preferred_element_type=f32)


def push(slots, rows, at, h_ref, adjoint_t, sums):
    listed, width = h_ref.shape[2:4]
    wide = jnp.concatenate(listed_blocks(h_ref, rows, at), axis=1)
    product = jnp.dot(adjoint_t, wide, preferred_element_type=f32)
    for k in range(listed):
        sums[slots[at * listed + k]] += product[:, k * width : (k + 1) * width]


def finish_push(sums, far_ref, near_ref, own_ref, across_ref):
    far_ref[...] = sums[0:4].astype(bf16)
    near_ref[...] = sums[12:16].astype(bf16)
    for at in range(4):
        own_ref[at] = sums[OWN[at]]
        across_ref[at] = sums[ACROSS[at]]


def first_kernel(
    top, rows, slots, place, coef, seeds_ref, h_hbm, cot_hbm,
    start_ref, term_ref, rounded_ref, cot_t_ref, adjoint_ref, far_ref, near_ref, own_ref, across_ref,
    h_ref, cot_ref, sums, h_sem, cot_sem,
):
    copies = []
    for at in range(4):
        source = (rows[at // 2], at % 2)
        copies.append(
            (
                pltpu.make_async_copy(h_hbm.at[source], h_ref.at[source], h_sem.at[at]),
                pltpu.make_async_copy(cot_hbm.at[source], cot_ref.at[at], cot_sem.at[at]),
            )
        )
    for pair in copies:
        for copy in pair:
            copy.start()
    for slot in range(16):
        start_ref[slot] = start_signs(place[slot], seeds_ref[...], h_ref.shape[3])
    sums[...] = jnp.zeros_like(sums)
    for at in range(4):
        copies[at][0].wait()
        value = window_product(slots, rows, at, h_ref, start_ref)
        term_ref[at] = value
        rounded_ref[at] = value.astype(bf16)
    for at in range(4):
        copies[at][1].wait()
        cot = cot_ref[at].astype(f32)
        cot_t = jnp.transpose(cot)
        cot_t_ref[at] = cot_t.astype(bf16)
        adjoint_ref[at] = (coef[top] * cot).astype(bf16)
        push(slots, rows, at, h_ref, (coef[top] * cot_t).astype(bf16), sums)
    finish_push(sums, far_ref, near_ref, own_ref, across_ref)


def forward_kernel(index, rows, slots, coef, h_ref, window, before_ref, sums_ref, term_ref, rounded_ref, density_ref):
    for at in range(4):
        before = (before_ref[OWN[at]] if index == 2 else before_ref[at]).astype(f32)
        value = 2.0 * window_product(slots, rows, at, h_ref, window) - before
        sums = coef[0] * before + coef[1] * sums_ref[at] if index == 2 else sums_ref[at]
        term_ref[at] = value
        rounded_ref[at] = value.astype(bf16)
        density_ref[at] = sums + coef[index] * value


def adjoint_value(at, index, coef, cot_t_ref, own_ref, far_ref, near_ref, across_ref):
    came = far_ref[at] if at < 2 else near_ref[at - 2]
    carried = own_ref[at] + came.astype(f32) + across_ref[at].astype(f32)
    return coef[index] * cot_t_ref[at].astype(f32) + 2.0 * carried


def adjoint_kernel(
    index, top, rows, slots, coef, h_ref, cot_t_ref, own_in, far_in, near_in, across_in,
    value_ref, rounded_ref, far_ref, near_ref, own_ref, across_ref, sums,
):
    sums[...] = jnp.zeros_like(sums)
    for at in range(4):
        value = adjoint_value(at, index, coef, cot_t_ref, own_in, far_in, near_in, across_in)
        if index + 2 == top:
            value = value - coef[top] * cot_t_ref[at].astype(f32)
        value_ref[at] = value
        push(slots, rows, at, h_ref, value.astype(bf16), sums)
        rounded_ref[at] = jnp.transpose(value).astype(bf16)
    finish_push(sums, far_ref, near_ref, own_ref, across_ref)


def block_gradients(slots, at, left, windows, listed, store):
    for k in range(listed):
        slot = slots[at * listed + k]
        right = jnp.concatenate([window[slot] for window in windows], axis=1)
        store(k, lax.dot_general(left, right, (((1,), (1,)), ((), ())), preferred_element_type=f32))


def early_gradient_kernel(terms, rows, slots, coef, cot_t_ref, own_ref, far_ref, near_ref, across_ref, older_ref, *rest):
    adjoints, windows, sums_ref = rest[: terms - 3], rest[terms - 3 : -1], rest[-1]
    listed = sums_ref.shape[1]
    for at in range(4):
        value = adjoint_value(at, 1, coef, cot_t_ref, own_ref, far_ref, near_ref, across_ref) - older_ref[at]
        left = [jnp.transpose(value).astype(bf16)] + [a[at] * bf16(2.0) for a in adjoints]

        def store(k, total, at=at):
            sums_ref[at, k] = total

        block_gradients(slots, at, jnp.concatenate(left, axis=1), windows, listed, store)


def last_kernel(
    index, scale, rows, slots, coef, h_ref, window, before_ref, sums_ref, adjoint_ref, early_ref,
    density_hbm, grad_hbm, density, grad, density_sem, grad_sem,
):
    listed = h_ref.shape[2]
    copies = []
    for at in range(4):
        place = (rows[at // 2], at % 2)
        value = 2.0 * window_product(slots, rows, at, h_ref, window) - before_ref[at]
        density[at] = sums_ref[at] + coef[index] * value
        copies.append(pltpu.make_async_copy(density.at[at], density_hbm.at[place], density_sem.at[at]))
        copies[-1].start()

        def store(k, total, at=at):
            grad[at, k] = ((early_ref[at, k] + total) * scale).astype(bf16)

        block_gradients(slots, at, adjoint_ref[at] * bf16(2.0), (window,), listed, store)
        copies.append(pltpu.make_async_copy(grad.at[at], grad_hbm.at[place], grad_sem.at[at]))
        copies[-1].start()
    for copy in copies:
        copy.wait()


def pair_shards(hamiltonian, neighbours, probe_seeds, coefficients, cotangent):
    rows_x, rows_y, listed, width = hamiltonian.shape[:4]
    probes = cotangent.shape[3]
    terms = coefficients.shape[0]
    top = terms - 1
    blocks = rows_x * rows_y
    span_x = rows_x * lax.axis_size("gx")
    span_y = rows_y * lax.axis_size("gy")
    odd = lax.axis_index("gx") % 2
    four = jnp.arange(4, dtype=jnp.int32)
    local_row = jnp.where(odd == 0, four - 1, 2 - four)
    place_x = (lax.axis_index("gx") * rows_x + local_row) % span_x
    place_y = (lax.axis_index("gy") * rows_y + four) % span_y
    place = ((place_x[:, None] * span_y + place_y) * width).reshape(-1).astype(jnp.int32)
    rows = jnp.stack([odd, 1 - odd]).astype(jnp.int32)
    codes = jnp.where(odd == 0, neighbours, neighbours[::-1])
    window_row = 1 + jnp.arange(2, dtype=jnp.int32)[:, None, None] + (1 - 2 * odd) * (codes // 3 - 1)
    window_col = (jnp.arange(2, dtype=jnp.int32)[None, :, None] + codes % 3 - 1) % 4
    slots = (window_row * 4 + window_col).reshape(-1).astype(jnp.int32)

    vmem = pl.BlockSpec(memory_space=pltpu.VMEM)
    smem = pl.BlockSpec(memory_space=pltpu.SMEM)
    outside = pl.BlockSpec(memory_space=pl.ANY)

    def field(count, dtype):
        return jax.ShapeDtypeStruct((count, width, probes), dtype)

    def turned(count, dtype):
        return jax.ShapeDtypeStruct((count, probes, width), dtype)

    apply_flops = 2 * blocks * listed * width * width * probes
    pushed = [turned(4, bf16), turned(4, bf16), turned(4, f32), turned(4, f32)]
    sums_scratch = pltpu.VMEM((16, probes, width), f32)

    def call(name, kernel, scalars, operands, out_shape, scratch=(), flops=apply_flops, out_specs=None, in_specs=None):
        return pl.pallas_call(
            kernel,
            in_specs=[smem] * len(scalars) + (in_specs or [vmem] * len(operands)),
            out_specs=out_specs or [vmem] * len(out_shape),
            out_shape=out_shape,
            scratch_shapes=list(scratch),
            compiler_params=pltpu.CompilerParams(vmem_limit_bytes=VMEM_BYTES),
            cost_estimate=pl.CostEstimate(flops=flops, bytes_accessed=2 * 1024 * 1024, transcendentals=0),
            name=name,
        )(*scalars, *operands)

    scalars = (rows, slots, coefficients)
    start, term, rounded, cot_t, adjoint, *sent = call(
        "first",
        functools.partial(first_kernel, top),
        (rows, slots, place, coefficients),
        (probe_seeds.reshape(1, probes), hamiltonian, cotangent),
        [field(16, bf16), field(4, f32), field(4, bf16), turned(4, bf16), field(4, bf16)] + pushed,
        scratch=(
            pltpu.VMEM(hamiltonian.shape, bf16),
            pltpu.VMEM((4, width, probes), bf16),
            sums_scratch,
            pltpu.SemaphoreType.DMA((4,)),
            pltpu.SemaphoreType.DMA((4,)),
        ),
        flops=2 * apply_flops,
        in_specs=[vmem, outside, outside],
    )
    adjoints = {top: adjoint}
    values = {}
    windows = [start]
    before, sums = start, term
    for index in range(2, terms):
        across = swap_y(rounded)
        outer = jnp.concatenate([rounded[:2], across[:2]])
        inner = jnp.concatenate([rounded[2:], across[2:]])
        window = jnp.concatenate([swap_far(outer), outer, inner, swap_near(inner)])
        to_far, to_near, own, to_across = sent
        far, near = swap_far(to_far), swap_near(to_near)
        to_across = to_across + jnp.concatenate([far[2:], near[2:]]).astype(f32)
        arrived = (cot_t, own, far, near, swap_y(to_across.astype(bf16)))

        windows.append(window)
        at = terms - index
        if index < top:
            following, rounded, density = call(
                "forward",
                functools.partial(forward_kernel, index),
                scalars, (hamiltonian, window, before, sums),
                [field(4, f32), field(4, bf16), field(4, f32)],
            )
            before, sums, term = term, density, following
            values[at], adjoints[at], *sent = call(
                "adjoint",
                functools.partial(adjoint_kernel, at, top),
                scalars, (hamiltonian,) + arrived,
                [turned(4, f32), field(4, bf16)] + pushed,
                scratch=(sums_scratch,),
            )
    early = call(
        "early_gradient",
        functools.partial(early_gradient_kernel, terms),
        scalars,
        arrived + (values[3],) + tuple(adjoints[t] for t in range(2, top)) + tuple(windows[: top - 1]),
        [jax.ShapeDtypeStruct((blocks, listed, width, width), f32)],
        flops=(terms - 2) * apply_flops,
    )[0]
    density, gradient = call(
        "last",
        functools.partial(last_kernel, top, 1.0 / probes),
        scalars, (hamiltonian, windows[top - 1], before, sums, adjoints[top], early),
        [
            jax.ShapeDtypeStruct(cotangent.shape, f32),
            jax.ShapeDtypeStruct(hamiltonian.shape, bf16),
        ],
        scratch=(
            pltpu.VMEM((4, width, probes), f32),
            pltpu.VMEM((blocks, listed, width, width), bf16),
            pltpu.SemaphoreType.DMA((4,)),
            pltpu.SemaphoreType.DMA((4,)),
        ),
        flops=2 * apply_flops,
        out_specs=[outside, outside],
    )
    return density, gradient


def shards(hamiltonian, neighbours, probe_seeds, coefficients, cotangent):
    paired = (
        hamiltonian.shape[:2] == (2, 2)
        and lax.axis_size("gy") == 2
        and lax.axis_size("gx") % 2 == 0
        and hamiltonian.shape[2] % 2 == 0
        and coefficients.shape[0] == 5
    )
    run = pair_shards if paired else any_shards
    return run(hamiltonian, neighbours, probe_seeds, coefficients, cotangent)


def solution(mesh):
    placed = (
        P("gx", "gy", None, None, None),
        P("gx", "gy", None),
        P(),
        P(),
        P("gx", "gy", None, None),
    )
    return jax.shard_map(
        shards,
        mesh=mesh,
        in_specs=placed,
        out_specs=(P("gx", "gy", None, None), P("gx", "gy", None, None, None)),
        check_vma=False,
    )
```

```python
import functools

import jax
import jax.numpy as jnp
from jax import lax
from jax.experimental import pallas as pl
from jax.experimental.pallas import tpu as pltpu
from jax.sharding import PartitionSpec as P

offset_table = tuple(((offset_code // 3 - 1, offset_code % 3 - 1) for offset_code in range(9)))


def shifted(value, axis, steps):
    count = lax.axis_size(axis)
    pairs = [(source, (source + steps) % count) for source in range(count)]
    return lax.ppermute(value, axis, pairs)


def padded_2(block, sides, width):
    for axis, dim in sides:
        count = lax.axis_size(axis)
        forward = [(i, i + 1) for i in range(count - 1)]
        forward.append((count - 1, 0))
        backward = [(target, source) for source, target in forward]
        low = lax.ppermute(
            lax.slice_in_dim(block, block.shape[dim] - width, None, axis=dim), axis, forward
        )
        high = lax.ppermute(lax.slice_in_dim(block, 0, width, axis=dim), axis, backward)
        block = jnp.concatenate([low, block, high], axis=dim)
    return block


def probe_signs(global_rows, seed_values):
    hashed = global_rows[..., None] * jnp.int32(-1640531535)
    hashed = hashed ^ seed_values
    hashed = hashed ^ hashed >> 15
    hashed = hashed * jnp.int32(739982445)
    hashed = hashed ^ hashed >> 12
    parity = hashed >> 7 & 1
    return (1 - 2 * parity).astype(jnp.float32)


def by_offset(hamiltonian, neighbours):
    onehot = (neighbours[..., None] == jnp.arange(9, dtype=jnp.int32)).astype(jnp.bfloat16)
    picked = jnp.einsum(
        "abkc,abkxy->abcxy", onehot, hamiltonian, preferred_element_type=jnp.float32
    )
    return picked.astype(jnp.bfloat16)


def forward_apply(selected, padded):
    rows_x, rows_y = (selected.shape[0], selected.shape[1])
    summed = jnp.zeros((rows_x, rows_y, selected.shape[3], padded.shape[3]), jnp.float32)
    for offset_code, (step_x, step_y) in enumerate(offset_table):
        window = padded[1 + step_x : 1 + step_x + rows_x, 1 + step_y : 1 + step_y + rows_y]
        summed = summed + jnp.einsum(
            "abxy,abyp->abxp",
            selected[:, :, offset_code],
            window,
            preferred_element_type=jnp.float32,
        )
    return summed


def push_transpose(selected, adjoint_bf16):
    rows_x, rows_y = (selected.shape[0], selected.shape[1])
    gathered = jnp.zeros((rows_x + 2, rows_y + 2) + adjoint_bf16.shape[2:], jnp.float32)
    for offset_code, (step_x, step_y) in enumerate(offset_table):
        product = jnp.einsum(
            "abyx,abyp->abxp",
            selected[:, :, offset_code],
            adjoint_bf16,
            preferred_element_type=jnp.float32,
        )
        gathered = gathered + jnp.pad(
            product, ((1 + step_x, 1 - step_x), (1 + step_y, 1 - step_y), (0, 0), (0, 0))
        )
    for offset_by, source, target in ((-1, 0, rows_x), (1, rows_x + 1, 1)):
        moved = shifted(gathered[source], "gx", offset_by)
        gathered = gathered.at[target].add(moved)
    middle = gathered[1 : rows_x + 1]
    for offset_by, source, target in ((-1, 0, rows_y), (1, rows_y + 1, 1)):
        moved = shifted(middle[:, source], "gy", offset_by)
        middle = middle.at[:, target].add(moved)
    return middle[:, 1 : rows_y + 1]


def any_shards(hamiltonian, neighbours, probe_seeds, coefficients, cotangent):
    rows_x, rows_y = (hamiltonian.shape[0], hamiltonian.shape[1])
    width = hamiltonian.shape[3]
    probes = cotangent.shape[3]
    count_terms = coefficients.shape[0]
    span_x = rows_x * lax.axis_size("gx")
    span_y = rows_y * lax.axis_size("gy")
    place_x = (lax.axis_index("gx") * rows_x + jnp.arange(rows_x + 2, dtype=jnp.int32) - 1) % span_x
    place_y = (lax.axis_index("gy") * rows_y + jnp.arange(rows_y + 2, dtype=jnp.int32) - 1) % span_y
    orbital = jnp.arange(width, dtype=jnp.int32)
    global_rows = (place_x[:, None] * span_y + place_y[None, :])[:, :, None] * width + orbital[
        None, None, :
    ]
    start_padded = probe_signs(global_rows, probe_seeds)
    start_term = start_padded[1 : rows_x + 1, 1 : rows_y + 1]
    selected = by_offset(hamiltonian, neighbours)
    term_pads = [start_padded.astype(jnp.bfloat16)]
    previous = start_term
    current = forward_apply(selected, term_pads[0])
    density = coefficients[0] * start_term + coefficients[1] * current
    for index in range(2, count_terms):
        padded = padded_2(current.astype(jnp.bfloat16), (("gx", 0), ("gy", 1)), 1)
        term_pads.append(padded)
        following = 2.0 * forward_apply(selected, padded) - previous
        previous, current = (current, following)
        density = density + coefficients[index] * current
    seed_field = cotangent.astype(jnp.float32)
    adjoints = {}
    adjoint_rounded = {}
    for index in range(count_terms - 1, 0, -1):
        value = coefficients[index] * seed_field
        if index + 1 < count_terms:
            carried = push_transpose(selected, adjoint_rounded[index + 1])
            value = value + 2.0 * carried
        if index + 2 < count_terms:
            value = value - adjoints[index + 2]
        adjoints[index] = value
        adjoint_rounded[index] = value.astype(jnp.bfloat16)
    adjoint_stack = jnp.concatenate(
        [adjoint_rounded[index] * (1.0 if index == 1 else 2.0) for index in range(1, count_terms)],
        axis=3,
    )
    term_stack = jnp.concatenate(term_pads, axis=3)
    gradient = jnp.zeros(hamiltonian.shape, jnp.float32)
    for offset_code, (step_x, step_y) in enumerate(offset_table):
        window = term_stack[1 + step_x : 1 + step_x + rows_x, 1 + step_y : 1 + step_y + rows_y]
        block_grad = jnp.einsum(
            "abxq,abyq->abxy", adjoint_stack, window, preferred_element_type=jnp.float32
        )
        gradient = gradient + jnp.where(
            (neighbours == offset_code)[..., None, None], block_grad[:, :, None], 0.0
        )
    return (density, (gradient * (1.0 / probes)).astype(jnp.bfloat16))


bf16 = jnp.bfloat16
f32 = jnp.float32
VMEM_BYTES = 16 * 1024 * 1024
OWN = (4, 5, 8, 9)
ACROSS = (6, 7, 10, 11)


def swap_y(value):
    return lax.ppermute(value, "gy", [(0, 1), (1, 0)])


def swap_near(value):
    count = lax.axis_size("gx")
    return lax.ppermute(value, "gx", [(i, i ^ 1) for i in range(count)])


def swap_far(value):
    count = lax.axis_size("gx")
    pairs = [(i, (i + 1) % count if i % 2 else (i - 1) % count) for i in range(count)]
    return lax.ppermute(value, "gx", pairs)


def start_signs(rows_from, seeds, width):
    shape = (width, seeds.shape[1])
    hashed = (rows_from + lax.broadcasted_iota(jnp.int32, shape, 0)) * jnp.int32(-1640531535)
    hashed = hashed ^ seeds
    hashed = hashed ^ hashed >> 15
    hashed = hashed * jnp.int32(739982445)
    hashed = hashed ^ hashed >> 12
    return (1 - 2 * (hashed >> 7 & 1)).astype(f32).astype(bf16)


def listed_blocks(h_ref, rows, at):
    return [h_ref[rows[at // 2], at % 2, k] for k in range(h_ref.shape[2])]


def window_product(slots, rows, at, h_ref, window):
    listed = h_ref.shape[2]
    left = jnp.concatenate(listed_blocks(h_ref, rows, at), axis=1)
    right = jnp.concatenate([window[slots[at * listed + k]] for k in range(listed)], axis=0)
    return jnp.dot(left, right, preferred_element_type=f32)


def push(slots, rows, at, h_ref, adjoint_t, sums):
    listed, width = h_ref.shape[2:4]
    wide = jnp.concatenate(listed_blocks(h_ref, rows, at), axis=1)
    product = jnp.dot(adjoint_t, wide, preferred_element_type=f32)
    for k in range(listed):
        sums[slots[at * listed + k]] += product[:, k * width : (k + 1) * width]


def finish_push(sums, far_ref, near_ref, own_ref, across_ref):
    far_ref[...] = sums[0:4].astype(bf16)
    near_ref[...] = sums[12:16].astype(bf16)
    for at in range(4):
        own_ref[at] = sums[OWN[at]]
        across_ref[at] = sums[ACROSS[at]]


def fill_window(parts, window):
    for at, part in enumerate(parts):
        window[4 * at : 4 * at + 4] = part[...]


def pack_rows_kernel(own_ref, across_ref, outer_ref, inner_ref):
    outer_ref[0:2] = own_ref[0:2]
    outer_ref[2:4] = across_ref[0:2]
    inner_ref[0:2] = own_ref[2:4]
    inner_ref[2:4] = across_ref[2:4]


def pack_across_kernel(across_ref, far_ref, near_ref, packed_ref):
    packed_ref[0:2] = (across_ref[0:2] + far_ref[2:4].astype(f32)).astype(bf16)
    packed_ref[2:4] = (across_ref[2:4] + near_ref[2:4].astype(f32)).astype(bf16)


def first_kernel(
    top, span_x, span_y, position, seeds_hbm, coef_hbm, codes_hbm, h_hbm, cot_hbm,
    start_ref, term_ref, rounded_ref, cot_t_ref, adjoint_ref, far_ref, near_ref, own_ref, across_ref,
    rows_out, slots_out, seeds_ref, coef, codes, h_ref, cot_ref, sums, small_sem, h_sem, cot_sem,
):
    gx, gy = position[0], position[1]
    odd = lax.rem(gx, 2)
    rows = (odd, 1 - odd)
    small = [
        pltpu.make_async_copy(source, target, small_sem.at[at])
        for at, (source, target) in enumerate(((seeds_hbm, seeds_ref), (codes_hbm, codes), (coef_hbm, coef)))
    ]
    for copy in small:
        copy.start()
    h_copies, cot_copies = [], []
    for at in range(4):
        source = (rows[at // 2], at % 2)
        h_copies.append(pltpu.make_async_copy(h_hbm.at[source], h_ref.at[source], h_sem.at[at]))
        cot_copies.append(pltpu.make_async_copy(cot_hbm.at[source], cot_ref.at[at], cot_sem.at[at]))
    for copy in h_copies + cot_copies:
        copy.start()
    sums[...] = jnp.zeros_like(sums)
    for copy in small:
        copy.wait()
    listed, width = h_ref.shape[2:4]
    for slot in range(16):
        local = jnp.where(odd == 0, slot // 4 - 1, 2 - slot // 4)
        place_x = lax.rem(gx * 2 + local + span_x, span_x)
        place_y = lax.rem(gy * 2 + slot % 4, span_y)
        start_ref[slot] = start_signs((place_x * span_y + place_y) * width, seeds_ref[...], width)
    slots = []
    for at in range(4):
        for k in range(listed):
            code = codes[rows[at // 2], at % 2, k]
            step_x = jnp.where(code >= 6, 1, jnp.where(code >= 3, 0, -1))
            step_y = code - 3 * step_x - 4
            slots.append((1 + at // 2 + (1 - 2 * odd) * step_x) * 4 + lax.rem(at % 2 + step_y + 4, 4))
    for at in range(2):
        rows_out[at] = rows[at]
    for at in range(4 * listed):
        slots_out[at] = slots[at]
    for at in range(4):
        h_copies[at].wait()
        value = window_product(slots, rows, at, h_ref, start_ref)
        term_ref[at] = value
        rounded_ref[at] = value.astype(bf16)
    for at in range(4):
        cot_copies[at].wait()
        cot = cot_ref[at].astype(f32)
        cot_t = jnp.transpose(cot)
        cot_t_ref[at] = cot_t.astype(bf16)
        adjoint_ref[at] = (coef[top] * cot).astype(bf16)
        push(slots, rows, at, h_ref, (coef[top] * cot_t).astype(bf16), sums)
    finish_push(sums, far_ref, near_ref, own_ref, across_ref)


def forward_kernel(
    index, rows, slots, coef, h_ref, far, outer, inner, near, before_ref, sums_ref, rounded_ref, density_ref, *rest
):
    term_ref, window = rest[:-1], rest[-1]
    fill_window((far, outer, inner, near), window)
    for at in range(4):
        before = (before_ref[OWN[at]] if index == 2 else before_ref[at]).astype(f32)
        value = 2.0 * window_product(slots, rows, at, h_ref, window) - before
        sums = coef[0] * before + coef[1] * sums_ref[at] if index == 2 else sums_ref[at]
        rounded_ref[at] = value.astype(bf16)
        density_ref[at] = sums + coef[index] * value
        for ref in term_ref:
            ref[at] = value


def adjoint_value(at, index, coef, cot_t_ref, own_ref, far_ref, near_ref, across_ref):
    came = far_ref[at] if at < 2 else near_ref[at - 2]
    carried = own_ref[at] + came.astype(f32) + across_ref[at].astype(f32)
    return coef[index] * cot_t_ref[at].astype(f32) + 2.0 * carried


def adjoint_kernel(
    index, top, rows, slots, coef, h_ref, cot_t_ref, own_in, far_in, near_in, across_in,
    rounded_ref, far_ref, near_ref, own_ref, across_ref, *rest,
):
    value_refs, sums = rest[:-1], rest[-1]
    sums[...] = jnp.zeros_like(sums)
    for at in range(4):
        value = adjoint_value(at, index, coef, cot_t_ref, own_in, far_in, near_in, across_in)
        if index + 2 == top:
            value = value - coef[top] * cot_t_ref[at].astype(f32)
        for ref in value_refs:
            ref[at] = value
        push(slots, rows, at, h_ref, value.astype(bf16), sums)
        rounded_ref[at] = jnp.transpose(value).astype(bf16)
    finish_push(sums, far_ref, near_ref, own_ref, across_ref)


def block_gradients(slots, at, left, windows, listed, store):
    for k in range(listed):
        slot = slots[at * listed + k]
        right = jnp.concatenate([window[slot] for window in windows], axis=1)
        store(k, lax.dot_general(left, right, (((1,), (1,)), ((), ())), preferred_element_type=f32))


def middle_gradient_kernel(count, slots, *refs):
    adjoints, parts, (sums_ref, windows) = refs[:count], refs[count : 5 * count], refs[5 * count :]
    listed = sums_ref.shape[1]
    for t in range(count):
        fill_window(parts[4 * t : 4 * t + 4], windows.at[t])
    for at in range(4):
        left = jnp.concatenate([a[at] * bf16(2.0) for a in adjoints], axis=1)

        def store(k, total, at=at):
            sums_ref[at, k] = total

        block_gradients(slots, at, left, [windows.at[t] for t in range(count)], listed, store)


def first_gradient_kernel(
    slots, coef, cot_t_ref, own_ref, far_ref, near_ref, across_ref, older_ref, start_ref, before_ref, sums_ref
):
    listed = sums_ref.shape[1]
    for at in range(4):
        value = adjoint_value(at, 1, coef, cot_t_ref, own_ref, far_ref, near_ref, across_ref) - older_ref[at]

        def store(k, total, at=at):
            sums_ref[at, k] = before_ref[at, k] + total

        block_gradients(slots, at, jnp.transpose(value).astype(bf16), (start_ref,), listed, store)


def last_kernel(
    index, scale, rows, slots, coef, h_ref, far, outer, inner, near, before_ref, sums_ref, adjoint_ref, early_ref,
    density_hbm, grad_hbm, density, grad, window, density_sem, grad_sem,
):
    fill_window((far, outer, inner, near), window)
    listed = h_ref.shape[2]
    copies = []
    for at in range(4):
        place = (rows[at // 2], at % 2)
        value = 2.0 * window_product(slots, rows, at, h_ref, window) - before_ref[at]
        density[at] = sums_ref[at] + coef[index] * value
        copies.append(pltpu.make_async_copy(density.at[at], density_hbm.at[place], density_sem.at[at]))
        copies[-1].start()

        def store(k, total, at=at):
            grad[at, k] = ((early_ref[at, k] + total) * scale).astype(bf16)

        block_gradients(slots, at, adjoint_ref[at] * bf16(2.0), (window,), listed, store)
        copies.append(pltpu.make_async_copy(grad.at[at], grad_hbm.at[place], grad_sem.at[at]))
        copies[-1].start()
    for copy in copies:
        copy.wait()


def pair_shards(hamiltonian, neighbours, probe_seeds, coefficients, cotangent):
    rows_x, rows_y, listed, width = hamiltonian.shape[:4]
    probes = cotangent.shape[3]
    terms = coefficients.shape[0]
    top = terms - 1
    blocks = rows_x * rows_y
    span_x = rows_x * lax.axis_size("gx")
    span_y = rows_y * lax.axis_size("gy")
    vmem = pl.BlockSpec(memory_space=pltpu.VMEM)
    smem = pl.BlockSpec(memory_space=pltpu.SMEM)
    hbm = pl.BlockSpec(memory_space=pltpu.HBM)

    def field(count, dtype):
        return jax.ShapeDtypeStruct((count, width, probes), dtype)

    def turned(count, dtype):
        return jax.ShapeDtypeStruct((count, probes, width), dtype)

    apply_flops = 2 * blocks * listed * width * width * probes
    pushed = [turned(4, bf16), turned(4, bf16), turned(4, f32), turned(4, f32)]
    sums_scratch = pltpu.VMEM((16, probes, width), f32)

    window_scratch = pltpu.VMEM((16, width, probes), bf16)

    def kept(values):
        return tuple(pltpu.with_memory_space_constraint(value, pltpu.VMEM) for value in values)

    def call(name, kernel, scalars, operands, out_shape, scratch=(), flops=apply_flops, out_specs=None, in_specs=None):
        return pl.pallas_call(
            kernel,
            in_specs=[smem] * len(scalars) + (in_specs or [vmem] * len(operands)),
            out_specs=out_specs or [vmem] * len(out_shape),
            out_shape=out_shape,
            scratch_shapes=list(scratch),
            compiler_params=pltpu.CompilerParams(vmem_limit_bytes=VMEM_BYTES),
            cost_estimate=pl.CostEstimate(flops=flops, bytes_accessed=2 * 1024 * 1024, transcendentals=0),
            name=name,
        )(*scalars, *operands)

    start, term, rounded, cot_t, adjoint, *sent, rows, slots = call(
        "first",
        functools.partial(first_kernel, top, span_x, span_y),
        (jnp.stack([lax.axis_index("gx"), lax.axis_index("gy")]).astype(jnp.int32),),
        tuple(
            pltpu.with_memory_space_constraint(value, pltpu.HBM)
            for value in (probe_seeds.reshape(1, probes), coefficients, neighbours, hamiltonian, cotangent)
        ),
        [field(16, bf16), field(4, f32), field(4, bf16), turned(4, bf16), field(4, bf16)]
        + pushed
        + [jax.ShapeDtypeStruct((2,), jnp.int32), jax.ShapeDtypeStruct((blocks * listed,), jnp.int32)],
        out_specs=[vmem] * 9 + [smem] * 2,
        scratch=(
            pltpu.VMEM((1, probes), jnp.int32),
            pltpu.SMEM(coefficients.shape, f32),
            pltpu.SMEM(neighbours.shape, jnp.int32),
            pltpu.VMEM(hamiltonian.shape, bf16),
            pltpu.VMEM((4, width, probes), bf16),
            sums_scratch,
            pltpu.SemaphoreType.DMA((3,)),
            pltpu.SemaphoreType.DMA((4,)),
            pltpu.SemaphoreType.DMA((4,)),
        ),
        flops=2 * apply_flops,
        in_specs=[hbm] * 5,
    )
    scalars = (rows, slots, coefficients)
    adjoints = {top: adjoint}
    windows = [(start,)]
    before, sums = start, term
    for index in range(2, terms):
        at = terms - index
        outer, inner = call(
            "pack_rows", pack_rows_kernel, (), kept((rounded, swap_y(rounded))), [field(4, bf16)] * 2, flops=0
        )
        far, near = swap_far(outer), swap_near(inner)
        to_far, to_near, own, to_across = sent
        from_far, from_near = swap_far(to_far), swap_near(to_near)
        (to_across,) = call(
            "pack_across", pack_across_kernel, (), kept((to_across, from_far, from_near)), [turned(4, bf16)], flops=0
        )
        from_across, _ = lax.optimization_barrier((swap_y(to_across), near))
        arrived = kept((cot_t, own, from_far, from_near, from_across))
        window = kept((far, outer, inner, near))
        windows.append(window)
        if index == top:
            break
        rounded, density, *following = call(
            "forward",
            functools.partial(forward_kernel, index),
            scalars, (hamiltonian,) + window + kept((before, sums)),
            [field(4, bf16), field(4, f32)] + [field(4, f32)] * (index + 2 <= top),
            scratch=(window_scratch,),
        )
        before, sums = term, density
        if following:
            term = following[0]
        adjoints[at], *sent = call(
            "adjoint",
            functools.partial(adjoint_kernel, at, top),
            scalars, (hamiltonian,) + arrived,
            [field(4, bf16)] + pushed + [turned(4, f32)] * (at == 3),
            scratch=(sums_scratch,),
        )
        if at == 3:
            older = sent.pop()
    gradient_sums = jax.ShapeDtypeStruct((blocks, listed, width, width), f32)
    middle = call(
        "middle_gradient",
        functools.partial(middle_gradient_kernel, terms - 3),
        (slots,), tuple(adjoints[t] for t in range(2, top)) + windows[1] + windows[2],
        [gradient_sums],
        scratch=(pltpu.VMEM((terms - 3, 16, width, probes), bf16),),
        flops=(terms - 3) * apply_flops,
    )[0]
    early = call(
        "first_gradient",
        first_gradient_kernel,
        (slots, coefficients), arrived + (older, start, middle),
        [gradient_sums],
    )[0]
    density, gradient = call(
        "last",
        functools.partial(last_kernel, top, 1.0 / probes),
        scalars, (hamiltonian,) + windows[top - 1] + kept((before, sums, adjoints[top], early)),
        [
            jax.ShapeDtypeStruct(cotangent.shape, f32),
            jax.ShapeDtypeStruct(hamiltonian.shape, bf16),
        ],
        scratch=(
            pltpu.VMEM((4, width, probes), f32),
            pltpu.VMEM((blocks, listed, width, width), bf16),
            window_scratch,
            pltpu.SemaphoreType.DMA((4,)),
            pltpu.SemaphoreType.DMA((4,)),
        ),
        flops=2 * apply_flops,
        out_specs=[hbm, hbm],
    )
    return density, gradient


def shards(hamiltonian, neighbours, probe_seeds, coefficients, cotangent):
    paired = (
        hamiltonian.shape[:2] == (2, 2)
        and lax.axis_size("gy") == 2
        and lax.axis_size("gx") % 2 == 0
        and hamiltonian.shape[2] % 2 == 0
        and coefficients.shape[0] == 5
    )
    run = pair_shards if paired else any_shards
    return run(hamiltonian, neighbours, probe_seeds, coefficients, cotangent)


def solution(mesh):
    placed = (
        P("gx", "gy", None, None, None),
        P("gx", "gy", None),
        P(),
        P(),
        P("gx", "gy", None, None),
    )
    return jax.shard_map(
        shards,
        mesh=mesh,
        in_specs=placed,
        out_specs=(P("gx", "gy", None, None), P("gx", "gy", None, None, None)),
        check_vma=False,
    )
```

```python
import functools

import jax
import jax.numpy as jnp
from jax import lax
from jax.experimental import pallas as pl
from jax.experimental.pallas import tpu as pltpu
from jax.sharding import PartitionSpec as P

offset_table = tuple(((offset_code // 3 - 1, offset_code % 3 - 1) for offset_code in range(9)))


def shifted(value, axis, steps):
    count = lax.axis_size(axis)
    pairs = [(source, (source + steps) % count) for source in range(count)]
    return lax.ppermute(value, axis, pairs)


def padded_2(block, sides, width):
    for axis, dim in sides:
        count = lax.axis_size(axis)
        forward = [(i, i + 1) for i in range(count - 1)]
        forward.append((count - 1, 0))
        backward = [(target, source) for source, target in forward]
        low = lax.ppermute(
            lax.slice_in_dim(block, block.shape[dim] - width, None, axis=dim), axis, forward
        )
        high = lax.ppermute(lax.slice_in_dim(block, 0, width, axis=dim), axis, backward)
        block = jnp.concatenate([low, block, high], axis=dim)
    return block


def probe_signs(global_rows, seed_values):
    hashed = global_rows[..., None] * jnp.int32(-1640531535)
    hashed = hashed ^ seed_values
    hashed = hashed ^ hashed >> 15
    hashed = hashed * jnp.int32(739982445)
    hashed = hashed ^ hashed >> 12
    parity = hashed >> 7 & 1
    return (1 - 2 * parity).astype(jnp.float32)


def by_offset(hamiltonian, neighbours):
    onehot = (neighbours[..., None] == jnp.arange(9, dtype=jnp.int32)).astype(jnp.bfloat16)
    picked = jnp.einsum(
        "abkc,abkxy->abcxy", onehot, hamiltonian, preferred_element_type=jnp.float32
    )
    return picked.astype(jnp.bfloat16)


def forward_apply(selected, padded):
    rows_x, rows_y = (selected.shape[0], selected.shape[1])
    summed = jnp.zeros((rows_x, rows_y, selected.shape[3], padded.shape[3]), jnp.float32)
    for offset_code, (step_x, step_y) in enumerate(offset_table):
        window = padded[1 + step_x : 1 + step_x + rows_x, 1 + step_y : 1 + step_y + rows_y]
        summed = summed + jnp.einsum(
            "abxy,abyp->abxp",
            selected[:, :, offset_code],
            window,
            preferred_element_type=jnp.float32,
        )
    return summed


def push_transpose(selected, adjoint_bf16):
    rows_x, rows_y = (selected.shape[0], selected.shape[1])
    gathered = jnp.zeros((rows_x + 2, rows_y + 2) + adjoint_bf16.shape[2:], jnp.float32)
    for offset_code, (step_x, step_y) in enumerate(offset_table):
        product = jnp.einsum(
            "abyx,abyp->abxp",
            selected[:, :, offset_code],
            adjoint_bf16,
            preferred_element_type=jnp.float32,
        )
        gathered = gathered + jnp.pad(
            product, ((1 + step_x, 1 - step_x), (1 + step_y, 1 - step_y), (0, 0), (0, 0))
        )
    for offset_by, source, target in ((-1, 0, rows_x), (1, rows_x + 1, 1)):
        moved = shifted(gathered[source], "gx", offset_by)
        gathered = gathered.at[target].add(moved)
    middle = gathered[1 : rows_x + 1]
    for offset_by, source, target in ((-1, 0, rows_y), (1, rows_y + 1, 1)):
        moved = shifted(middle[:, source], "gy", offset_by)
        middle = middle.at[:, target].add(moved)
    return middle[:, 1 : rows_y + 1]


def any_shards(hamiltonian, neighbours, probe_seeds, coefficients, cotangent):
    rows_x, rows_y = (hamiltonian.shape[0], hamiltonian.shape[1])
    width = hamiltonian.shape[3]
    probes = cotangent.shape[3]
    count_terms = coefficients.shape[0]
    span_x = rows_x * lax.axis_size("gx")
    span_y = rows_y * lax.axis_size("gy")
    place_x = (lax.axis_index("gx") * rows_x + jnp.arange(rows_x + 2, dtype=jnp.int32) - 1) % span_x
    place_y = (lax.axis_index("gy") * rows_y + jnp.arange(rows_y + 2, dtype=jnp.int32) - 1) % span_y
    orbital = jnp.arange(width, dtype=jnp.int32)
    global_rows = (place_x[:, None] * span_y + place_y[None, :])[:, :, None] * width + orbital[
        None, None, :
    ]
    start_padded = probe_signs(global_rows, probe_seeds)
    start_term = start_padded[1 : rows_x + 1, 1 : rows_y + 1]
    selected = by_offset(hamiltonian, neighbours)
    term_pads = [start_padded.astype(jnp.bfloat16)]
    previous = start_term
    current = forward_apply(selected, term_pads[0])
    density = coefficients[0] * start_term + coefficients[1] * current
    for index in range(2, count_terms):
        padded = padded_2(current.astype(jnp.bfloat16), (("gx", 0), ("gy", 1)), 1)
        term_pads.append(padded)
        following = 2.0 * forward_apply(selected, padded) - previous
        previous, current = (current, following)
        density = density + coefficients[index] * current
    seed_field = cotangent.astype(jnp.float32)
    adjoints = {}
    adjoint_rounded = {}
    for index in range(count_terms - 1, 0, -1):
        value = coefficients[index] * seed_field
        if index + 1 < count_terms:
            carried = push_transpose(selected, adjoint_rounded[index + 1])
            value = value + 2.0 * carried
        if index + 2 < count_terms:
            value = value - adjoints[index + 2]
        adjoints[index] = value
        adjoint_rounded[index] = value.astype(jnp.bfloat16)
    adjoint_stack = jnp.concatenate(
        [adjoint_rounded[index] * (1.0 if index == 1 else 2.0) for index in range(1, count_terms)],
        axis=3,
    )
    term_stack = jnp.concatenate(term_pads, axis=3)
    gradient = jnp.zeros(hamiltonian.shape, jnp.float32)
    for offset_code, (step_x, step_y) in enumerate(offset_table):
        window = term_stack[1 + step_x : 1 + step_x + rows_x, 1 + step_y : 1 + step_y + rows_y]
        block_grad = jnp.einsum(
            "abxq,abyq->abxy", adjoint_stack, window, preferred_element_type=jnp.float32
        )
        gradient = gradient + jnp.where(
            (neighbours == offset_code)[..., None, None], block_grad[:, :, None], 0.0
        )
    return (density, (gradient * (1.0 / probes)).astype(jnp.bfloat16))


bf16 = jnp.bfloat16
f32 = jnp.float32
VMEM_BYTES = 16 * 1024 * 1024
OWN = (4, 5, 8, 9)


def swap_y(value):
    return lax.ppermute(value, "gy", [(0, 1), (1, 0)])


def swap_near(value):
    count = lax.axis_size("gx")
    return lax.ppermute(value, "gx", [(i, i ^ 1) for i in range(count)])


def swap_far(value):
    count = lax.axis_size("gx")
    pairs = [(i, (i + 1) % count if i % 2 else (i - 1) % count) for i in range(count)]
    return lax.ppermute(value, "gx", pairs)


def start_signs(rows_from, seeds, width):
    shape = (width, seeds.shape[1])
    hashed = (rows_from + lax.broadcasted_iota(jnp.int32, shape, 0)) * jnp.int32(-1640531535)
    hashed = hashed ^ seeds
    hashed = hashed ^ hashed >> 15
    hashed = hashed * jnp.int32(739982445)
    hashed = hashed ^ hashed >> 12
    return jnp.where((hashed & 128) == 0, f32(1.0), f32(-1.0)).astype(bf16)


def step_of(code):
    return code // 3 - 1, code % 3 - 1


def window_product(at, coded, rows_of_blocks):
    right = []
    for code in range(9):
        step_x, step_y = step_of(code)
        right.append(rows_of_blocks[1 + at // 2 + step_x][(at % 2 + step_y) % 4])
    left = jnp.concatenate([coded[at, code] for code in range(9)], axis=1)
    return jnp.dot(left, jnp.concatenate(right, axis=0), preferred_element_type=f32)


def push(coded, fields, near_ref, own_ref, across_ref, far_ref):
    for col in range(4):
        sources = [(b, (col - b + 1) % 4 - 1) for b in range(2) if (col - b + 1) % 4 < 3]

        def blocks(row, *steps):
            return [
                jnp.concatenate([coded[2 * row + b, 3 * (step_x + 1) + step_y + 1] for step_x in steps], axis=1)
                for b, step_y in sources
            ]

        def total(rows, right):
            left = jnp.concatenate([fields[2 * row + b] for row in rows for b, _ in sources], axis=1)
            return jnp.dot(left, jnp.concatenate(right, axis=0), preferred_element_type=f32)

        far_ref[col] = total((0,), blocks(0, -1)).astype(bf16)
        near_ref[col] = total((1,), blocks(1, 1)).astype(bf16)
        middle = total((0, 1), blocks(0, 0, 1) + blocks(1, -1, 0))
        width = middle.shape[1] // 2
        ref = own_ref if col < 2 else across_ref
        ref[col % 2] = middle[:, :width]
        ref[2 + col % 2] = middle[:, width:]


def fill_window(parts, window):
    first = 0
    for part in parts:
        window[first : first + part.shape[0]] = part[...]
        first += part.shape[0]


def pack_rows_kernel(own_ref, across_ref, outer_ref, inner_ref):
    outer_ref[0:2] = own_ref[0:2]
    outer_ref[2:4] = across_ref[0:2]
    inner_ref[0:2] = own_ref[2:4]
    inner_ref[2:4] = across_ref[2:4]


def pack_across_kernel(across_ref, near_ref, far_ref, packed_ref):
    packed_ref[0:2] = (across_ref[0:2] + far_ref[2:4].astype(f32)).astype(bf16)
    packed_ref[2:4] = (across_ref[2:4] + near_ref[2:4].astype(f32)).astype(bf16)


def first_kernel(
    top, span_x, span_y, position, seeds_hbm, coef_hbm, codes_hbm, h_hbm, cot_hbm,
    rows_out, slots_out, coded, start_ref, term_ref, cot_t_ref, adjoint_ref, rounded_ref, *rest,
):
    sent_refs, (seeds_ref, coef, codes, h_ref, cot_ref, small_sem, h_sem, cot_sem) = rest[:-8], rest[-8:]
    gx, gy = position[0], position[1]
    odd = lax.rem(gx, 2)
    rows = (odd, 1 - odd)
    copies = [
        pltpu.make_async_copy(source, target, small_sem.at[at])
        for at, (source, target) in enumerate(((seeds_hbm, seeds_ref), (codes_hbm, codes), (coef_hbm, coef)))
    ]
    for at in range(4):
        source = (rows[at // 2], at % 2)
        copies.append(pltpu.make_async_copy(h_hbm.at[source], h_ref.at[at], h_sem.at[at]))
        copies.append(pltpu.make_async_copy(cot_hbm.at[source], cot_ref.at[at], cot_sem.at[at]))
    for copy in copies:
        copy.start()
    coded[...] = jnp.zeros_like(coded)
    for copy in copies[:3]:
        copy.wait()
    listed, width = h_ref.shape[1:3]
    places = []
    for at in range(4):
        for k in range(listed):
            code = codes[rows[at // 2], at % 2, k]
            step_x = jnp.where(code >= 6, 1, jnp.where(code >= 3, 0, -1))
            step_y = code - 3 * step_x - 4
            step_x = (1 - 2 * odd) * step_x
            places.append(3 * step_x + step_y + 4)
            slots_out[at * listed + k] = (1 + at // 2 + step_x) * 4 + lax.rem(at % 2 + step_y + 4, 4)
    for at in range(2):
        rows_out[at] = rows[at]
    for copy in copies[3:]:
        copy.wait()
    for at in range(4):
        for k in range(listed):
            coded[at, places[at * listed + k]] = h_ref[at, k]
    fields = []
    for at in range(4):
        cot = cot_ref[at].astype(f32)
        cot_t = jnp.transpose(cot)
        cot_t_ref[at] = cot_t.astype(bf16)
        adjoint_ref[at] = (coef[top] * cot).astype(bf16)
        fields.append((coef[top] * cot_t).astype(bf16))
    for slot in range(16):
        local = jnp.where(odd == 0, slot // 4 - 1, 2 - slot // 4)
        place_x = lax.rem(gx * 2 + local + span_x, span_x)
        place_y = lax.rem(gy * 2 + slot % 4, span_y)
        start_ref[slot] = start_signs((place_x * span_y + place_y) * width, seeds_ref[...], width)
    push(coded, fields, *sent_refs)
    for at in range(4):
        value = window_product(at, coded, [start_ref.at[pl.ds(4 * row, 4)] for row in range(4)])
        term_ref[at] = value
        rounded_ref[at] = value.astype(bf16)


def forward_kernel(index, has_term, coef, coded, far, outer, inner, near, before_ref, sums_ref, density_ref, rounded_ref, *term_ref):
    for at in range(4):
        before = (before_ref[OWN[at]] if index == 2 else before_ref[at]).astype(f32)
        value = 2.0 * window_product(at, coded, (far, outer, inner, near)) - before
        sums = coef[0] * before + coef[1] * sums_ref[at] if index == 2 else sums_ref[at]
        rounded_ref[at] = value.astype(bf16)
        density_ref[at] = sums + coef[index] * value
        if has_term:
            term_ref[0][at] = value


def adjoint_value(at, index, coef, cot_t_ref, own_ref, across_ref, near_ref, far_ref):
    came = (far_ref if at < 2 else near_ref)[at % 2]
    carried = own_ref[at] + across_ref[at].astype(f32) + came.astype(f32)
    return coef[index] * cot_t_ref[at].astype(f32) + 2.0 * carried


def adjoint_kernel(index, top, coef, coded, *refs):
    arrived, rounded_ref, sent_refs, value_refs = refs[:5], refs[5], refs[6:10], refs[10:]
    fields = []
    for at in range(4):
        value = adjoint_value(at, index, coef, *arrived)
        if index + 2 == top:
            value = value - coef[top] * arrived[0][at].astype(f32)
        for ref in value_refs:
            ref[at] = value
        fields.append(value.astype(bf16))
        rounded_ref[at] = fields[-1]
    push(coded, fields, *sent_refs)


def block_gradients(slots, at, left, windows, listed, store):
    for k in range(listed):
        slot = slots[at * listed + k]
        right = jnp.concatenate([window[slot] for window in windows], axis=1)
        store(k, lax.dot_general(left, right, (((1,), (1,)), ((), ())), preferred_element_type=f32))


def middle_gradient_kernel(parts, slots, *refs):
    count = len(parts)
    adjoints, (sums_ref, windows) = refs[:count], refs[-2:]
    listed = sums_ref.shape[1]
    first = count
    for t in range(count):
        fill_window(refs[first : first + parts[t]], windows.at[t])
        first += parts[t]
    for at in range(4):
        left = [jnp.transpose(2.0 * a[at].astype(f32)).astype(bf16) for a in adjoints]

        def store(k, total, at=at):
            sums_ref[at, k] = total

        block_gradients(slots, at, jnp.concatenate(left, axis=1), [windows.at[t] for t in range(count)], listed, store)


def first_gradient_kernel(slots, coef, older_ref, start_ref, before_ref, *refs):
    arrived, sums_ref = refs[:-1], refs[-1]
    listed = sums_ref.shape[1]
    for at in range(4):
        value = adjoint_value(at, 1, coef, *arrived) - older_ref[at]

        def store(k, total, at=at):
            sums_ref[at, k] = before_ref[at, k] + total

        block_gradients(slots, at, jnp.transpose(value).astype(bf16), (start_ref,), listed, store)


def last_kernel(index, scale, rows, slots, coef, coded, *refs):
    before_ref, sums_ref, adjoint_ref, early_ref, density_hbm, grad_hbm, density, grad, window, density_sem, grad_sem = refs[4:]
    fill_window(refs[:4], window)
    listed = early_ref.shape[1]
    copies = []
    for at in range(4):
        place = (rows[at // 2], at % 2)
        value = 2.0 * window_product(at, coded, refs[:4]) - before_ref[at]
        density[at] = sums_ref[at] + coef[index] * value
        copies.append(pltpu.make_async_copy(density.at[at], density_hbm.at[place], density_sem.at[at]))
        copies[-1].start()

        def store(k, total, at=at):
            grad[at, k] = ((early_ref[at, k] + total) * scale).astype(bf16)

        block_gradients(slots, at, adjoint_ref[at] * bf16(2.0), (window,), listed, store)
        copies.append(pltpu.make_async_copy(grad.at[at], grad_hbm.at[place], grad_sem.at[at]))
        copies[-1].start()
    for copy in copies:
        copy.wait()


def pair_shards(hamiltonian, neighbours, probe_seeds, coefficients, cotangent):
    rows_x, rows_y, listed, width = hamiltonian.shape[:4]
    probes = cotangent.shape[3]
    terms = coefficients.shape[0]
    top = terms - 1
    blocks = rows_x * rows_y
    span_x = rows_x * lax.axis_size("gx")
    span_y = rows_y * lax.axis_size("gy")
    vmem = pl.BlockSpec(memory_space=pltpu.VMEM)
    smem = pl.BlockSpec(memory_space=pltpu.SMEM)
    hbm = pl.BlockSpec(memory_space=pltpu.HBM)

    def field(count, dtype):
        return jax.ShapeDtypeStruct((count, width, probes), dtype)

    def turned(count, dtype):
        return jax.ShapeDtypeStruct((count, probes, width), dtype)

    apply_flops = 2 * blocks * listed * width * width * probes
    sent_shapes = [turned(4, bf16), turned(4, f32), turned(4, f32), turned(4, bf16)]
    window_scratch = pltpu.VMEM((16, width, probes), bf16)

    def kept(values):
        return tuple(pltpu.with_memory_space_constraint(value, pltpu.VMEM) for value in values)

    def call(name, kernel, scalars, operands, out_shape, scratch=(), flops=apply_flops, out_specs=None, in_specs=None):
        return pl.pallas_call(
            kernel,
            in_specs=[smem] * len(scalars) + (in_specs or [vmem] * len(operands)),
            out_specs=out_specs or [vmem] * len(out_shape),
            out_shape=out_shape,
            scratch_shapes=list(scratch),
            compiler_params=pltpu.CompilerParams(vmem_limit_bytes=VMEM_BYTES),
            cost_estimate=pl.CostEstimate(flops=flops, bytes_accessed=1024 * 1024, transcendentals=0),
            name=name,
        )(*scalars, *operands)

    gradient_sums = jax.ShapeDtypeStruct((blocks, listed, width, width), f32)
    shapes = [jax.ShapeDtypeStruct((2,), jnp.int32), jax.ShapeDtypeStruct((blocks * listed,), jnp.int32)]
    shapes += [jax.ShapeDtypeStruct((blocks, 9, width, width), bf16), field(16, bf16), field(4, f32)]
    shapes += [turned(4, bf16), field(4, bf16), field(4, bf16)] + sent_shapes
    rows, slots, coded, start, term, cot_t, adjoint, rounded, to_near, own, to_across, to_far = call(
        "first",
        functools.partial(first_kernel, top, span_x, span_y),
        (jnp.stack([lax.axis_index("gx"), lax.axis_index("gy")]).astype(jnp.int32),),
        tuple(
            pltpu.with_memory_space_constraint(value, pltpu.HBM)
            for value in (probe_seeds.reshape(1, probes), coefficients, neighbours, hamiltonian, cotangent)
        ),
        shapes,
        out_specs=[smem] * 2 + [vmem] * (len(shapes) - 2),
        scratch=(
            pltpu.VMEM((1, probes), jnp.int32),
            pltpu.SMEM(coefficients.shape, f32),
            pltpu.SMEM(neighbours.shape, jnp.int32),
            pltpu.VMEM((blocks, listed, width, width), bf16),
            pltpu.VMEM((blocks, width, probes), bf16),
            pltpu.SemaphoreType.DMA((3,)),
            pltpu.SemaphoreType.DMA((4,)),
            pltpu.SemaphoreType.DMA((4,)),
        ),
        flops=2 * apply_flops,
        in_specs=[hbm] * 5,
    )
    (coded,) = kept((coded,))
    adjoints = {top: adjoint}
    windows = []
    before, sums = start, term
    for index in range(2, terms):
        at = terms - index
        outer, inner = call(
            "pack_rows", pack_rows_kernel, (), kept((rounded, swap_y(rounded))), [field(4, bf16)] * 2, flops=0
        )
        near = swap_near(inner)
        window = kept((swap_far(outer), outer, inner, near))
        from_near, from_far = swap_near(to_near), swap_far(to_far)
        if index == top:
            middle = call(
                "middle_gradient",
                functools.partial(middle_gradient_kernel, (4,) * len(windows)),
                (slots,),
                kept(tuple(adjoints[t] for t in range(2, top)) + tuple(part for shown in windows for part in shown)),
                [gradient_sums],
                scratch=(pltpu.VMEM((terms - 3, 16, width, probes), bf16),),
                flops=(terms - 3) * apply_flops,
            )[0]
            from_near, middle = lax.optimization_barrier((from_near, middle))
        (to_across,) = call(
            "pack_across", pack_across_kernel, (), kept((to_across, from_near, from_far)), [turned(4, bf16)], flops=0
        )
        arrived = kept((cot_t, own, swap_y(to_across), from_near, from_far))
        if index == top:
            break
        windows.append(window)
        has_term = index + 2 <= top
        density, rounded, *following = call(
            "forward",
            functools.partial(forward_kernel, index, has_term),
            (coefficients,), (coded,) + window + kept((before, sums)),
            [field(4, f32), field(4, bf16)] + [field(4, f32)] * has_term,
        )
        before, sums = term, density
        term = following[0] if has_term else None
        has_value = at == 3
        adjoints[at], to_near, own, to_across, to_far, *rest = call(
            "adjoint",
            functools.partial(adjoint_kernel, at, top),
            (coefficients,), (coded,) + arrived,
            [turned(4, bf16)] + sent_shapes + [turned(4, f32)] * has_value,
        )
        if has_value:
            older = rest[0]
    early = call(
        "first_gradient",
        first_gradient_kernel,
        (slots, coefficients), kept((older, start, middle)) + arrived,
        [gradient_sums],
    )[0]
    density, gradient = call(
        "last",
        functools.partial(last_kernel, top, 1.0 / probes),
        (rows, slots, coefficients), (coded,) + window + kept((before, sums, adjoints[top], early)),
        [
            jax.ShapeDtypeStruct(cotangent.shape, f32),
            jax.ShapeDtypeStruct(hamiltonian.shape, bf16),
        ],
        scratch=(
            pltpu.VMEM((4, width, probes), f32),
            pltpu.VMEM((blocks, listed, width, width), bf16),
            window_scratch,
            pltpu.SemaphoreType.DMA((4,)),
            pltpu.SemaphoreType.DMA((4,)),
        ),
        flops=2 * apply_flops,
        out_specs=[hbm, hbm],
    )
    return density, gradient


def shards(hamiltonian, neighbours, probe_seeds, coefficients, cotangent):
    paired = (
        hamiltonian.shape[:2] == (2, 2)
        and lax.axis_size("gy") == 2
        and lax.axis_size("gx") % 2 == 0
        and hamiltonian.shape[2] % 2 == 0
        and coefficients.shape[0] == 5
    )
    run = pair_shards if paired else any_shards
    return run(hamiltonian, neighbours, probe_seeds, coefficients, cotangent)


def solution(mesh):
    placed = (
        P("gx", "gy", None, None, None),
        P("gx", "gy", None),
        P(),
        P(),
        P("gx", "gy", None, None),
    )
    return jax.shard_map(
        shards,
        mesh=mesh,
        in_specs=placed,
        out_specs=(P("gx", "gy", None, None), P("gx", "gy", None, None, None)),
        check_vma=False,
    )
```

```python
import functools

import jax
import jax.numpy as jnp
from jax import lax
from jax.experimental import pallas as pl
from jax.experimental.pallas import tpu as pltpu
from jax.sharding import PartitionSpec as P

offset_table = tuple(((offset_code // 3 - 1, offset_code % 3 - 1) for offset_code in range(9)))


def shifted(value, axis, steps):
    count = lax.axis_size(axis)
    pairs = [(source, (source + steps) % count) for source in range(count)]
    return lax.ppermute(value, axis, pairs)


def padded_2(block, sides, width):
    for axis, dim in sides:
        count = lax.axis_size(axis)
        forward = [(i, i + 1) for i in range(count - 1)]
        forward.append((count - 1, 0))
        backward = [(target, source) for source, target in forward]
        low = lax.ppermute(
            lax.slice_in_dim(block, block.shape[dim] - width, None, axis=dim), axis, forward
        )
        high = lax.ppermute(lax.slice_in_dim(block, 0, width, axis=dim), axis, backward)
        block = jnp.concatenate([low, block, high], axis=dim)
    return block


def probe_signs(global_rows, seed_values):
    hashed = global_rows[..., None] * jnp.int32(-1640531535)
    hashed = hashed ^ seed_values
    hashed = hashed ^ hashed >> 15
    hashed = hashed * jnp.int32(739982445)
    hashed = hashed ^ hashed >> 12
    parity = hashed >> 7 & 1
    return (1 - 2 * parity).astype(jnp.float32)


def by_offset(hamiltonian, neighbours):
    onehot = (neighbours[..., None] == jnp.arange(9, dtype=jnp.int32)).astype(jnp.bfloat16)
    picked = jnp.einsum(
        "abkc,abkxy->abcxy", onehot, hamiltonian, preferred_element_type=jnp.float32
    )
    return picked.astype(jnp.bfloat16)


def forward_apply(selected, padded):
    rows_x, rows_y = (selected.shape[0], selected.shape[1])
    summed = jnp.zeros((rows_x, rows_y, selected.shape[3], padded.shape[3]), jnp.float32)
    for offset_code, (step_x, step_y) in enumerate(offset_table):
        window = padded[1 + step_x : 1 + step_x + rows_x, 1 + step_y : 1 + step_y + rows_y]
        summed = summed + jnp.einsum(
            "abxy,abyp->abxp",
            selected[:, :, offset_code],
            window,
            preferred_element_type=jnp.float32,
        )
    return summed


def push_transpose(selected, adjoint_bf16):
    rows_x, rows_y = (selected.shape[0], selected.shape[1])
    gathered = jnp.zeros((rows_x + 2, rows_y + 2) + adjoint_bf16.shape[2:], jnp.float32)
    for offset_code, (step_x, step_y) in enumerate(offset_table):
        product = jnp.einsum(
            "abyx,abyp->abxp",
            selected[:, :, offset_code],
            adjoint_bf16,
            preferred_element_type=jnp.float32,
        )
        gathered = gathered + jnp.pad(
            product, ((1 + step_x, 1 - step_x), (1 + step_y, 1 - step_y), (0, 0), (0, 0))
        )
    for offset_by, source, target in ((-1, 0, rows_x), (1, rows_x + 1, 1)):
        moved = shifted(gathered[source], "gx", offset_by)
        gathered = gathered.at[target].add(moved)
    middle = gathered[1 : rows_x + 1]
    for offset_by, source, target in ((-1, 0, rows_y), (1, rows_y + 1, 1)):
        moved = shifted(middle[:, source], "gy", offset_by)
        middle = middle.at[:, target].add(moved)
    return middle[:, 1 : rows_y + 1]


def any_shards(hamiltonian, neighbours, probe_seeds, coefficients, cotangent):
    rows_x, rows_y = (hamiltonian.shape[0], hamiltonian.shape[1])
    width = hamiltonian.shape[3]
    probes = cotangent.shape[3]
    count_terms = coefficients.shape[0]
    span_x = rows_x * lax.axis_size("gx")
    span_y = rows_y * lax.axis_size("gy")
    place_x = (lax.axis_index("gx") * rows_x + jnp.arange(rows_x + 2, dtype=jnp.int32) - 1) % span_x
    place_y = (lax.axis_index("gy") * rows_y + jnp.arange(rows_y + 2, dtype=jnp.int32) - 1) % span_y
    orbital = jnp.arange(width, dtype=jnp.int32)
    global_rows = (place_x[:, None] * span_y + place_y[None, :])[:, :, None] * width + orbital[
        None, None, :
    ]
    start_padded = probe_signs(global_rows, probe_seeds)
    start_term = start_padded[1 : rows_x + 1, 1 : rows_y + 1]
    selected = by_offset(hamiltonian, neighbours)
    term_pads = [start_padded.astype(jnp.bfloat16)]
    previous = start_term
    current = forward_apply(selected, term_pads[0])
    density = coefficients[0] * start_term + coefficients[1] * current
    for index in range(2, count_terms):
        padded = padded_2(current.astype(jnp.bfloat16), (("gx", 0), ("gy", 1)), 1)
        term_pads.append(padded)
        following = 2.0 * forward_apply(selected, padded) - previous
        previous, current = (current, following)
        density = density + coefficients[index] * current
    seed_field = cotangent.astype(jnp.float32)
    adjoints = {}
    adjoint_rounded = {}
    for index in range(count_terms - 1, 0, -1):
        value = coefficients[index] * seed_field
        if index + 1 < count_terms:
            carried = push_transpose(selected, adjoint_rounded[index + 1])
            value = value + 2.0 * carried
        if index + 2 < count_terms:
            value = value - adjoints[index + 2]
        adjoints[index] = value
        adjoint_rounded[index] = value.astype(jnp.bfloat16)
    adjoint_stack = jnp.concatenate(
        [adjoint_rounded[index] * (1.0 if index == 1 else 2.0) for index in range(1, count_terms)],
        axis=3,
    )
    term_stack = jnp.concatenate(term_pads, axis=3)
    gradient = jnp.zeros(hamiltonian.shape, jnp.float32)
    for offset_code, (step_x, step_y) in enumerate(offset_table):
        window = term_stack[1 + step_x : 1 + step_x + rows_x, 1 + step_y : 1 + step_y + rows_y]
        block_grad = jnp.einsum(
            "abxq,abyq->abxy", adjoint_stack, window, preferred_element_type=jnp.float32
        )
        gradient = gradient + jnp.where(
            (neighbours == offset_code)[..., None, None], block_grad[:, :, None], 0.0
        )
    return (density, (gradient * (1.0 / probes)).astype(jnp.bfloat16))


bf16 = jnp.bfloat16
f32 = jnp.float32
VMEM_BYTES = 16 * 1024 * 1024
OWN = (4, 5, 8, 9)


def swap_y(value):
    return lax.ppermute(value, "gy", [(0, 1), (1, 0)])


def swap_near(value):
    count = lax.axis_size("gx")
    return lax.ppermute(value, "gx", [(i, i ^ 1) for i in range(count)])


def swap_far(value):
    count = lax.axis_size("gx")
    pairs = [(i, (i + 1) % count if i % 2 else (i - 1) % count) for i in range(count)]
    return lax.ppermute(value, "gx", pairs)


def start_signs(rows_from, seeds, width):
    shape = (width, seeds.shape[1])
    hashed = (rows_from + lax.broadcasted_iota(jnp.int32, shape, 0)) * jnp.int32(-1640531535)
    hashed = hashed ^ seeds
    hashed = hashed ^ hashed >> 15
    hashed = hashed * jnp.int32(739982445)
    hashed = hashed ^ hashed >> 12
    return jnp.where((hashed & 128) == 0, f32(1.0), f32(-1.0)).astype(bf16)


def step_of(code):
    return code // 3 - 1, code % 3 - 1


def window_product(at, coded, rows_of_blocks):
    right = []
    for code in range(9):
        step_x, step_y = step_of(code)
        right.append(rows_of_blocks[1 + at // 2 + step_x][(at % 2 + step_y) % 4])
    left = jnp.concatenate([coded[at, code] for code in range(9)], axis=1)
    return jnp.dot(left, jnp.concatenate(right, axis=0), preferred_element_type=f32)


def push(coded, fields, near_ref, own_ref, across_ref, far_ref):
    for col in range(4):
        sources = [(b, (col - b + 1) % 4 - 1) for b in range(2) if (col - b + 1) % 4 < 3]

        def blocks(row, *steps):
            return [
                jnp.concatenate([coded[2 * row + b, 3 * (step_x + 1) + step_y + 1] for step_x in steps], axis=1)
                for b, step_y in sources
            ]

        def total(rows, right):
            left = jnp.concatenate([fields[2 * row + b] for row in rows for b, _ in sources], axis=1)
            return jnp.dot(left, jnp.concatenate(right, axis=0), preferred_element_type=f32)

        far_ref[col] = total((0,), blocks(0, -1)).astype(bf16)
        near_ref[col] = total((1,), blocks(1, 1)).astype(bf16)
        middle = total((0, 1), blocks(0, 0, 1) + blocks(1, -1, 0))
        width = middle.shape[1] // 2
        ref = own_ref if col < 2 else across_ref
        ref[col % 2] = middle[:, :width]
        ref[2 + col % 2] = middle[:, width:]


def fill_window(parts, window):
    first = 0
    for part in parts:
        window[first : first + part.shape[0]] = part[...]
        first += part.shape[0]


def pack_rows_kernel(own_ref, across_ref, outer_ref, inner_ref):
    outer_ref[0:2] = own_ref[0:2]
    outer_ref[2:4] = across_ref[0:2]
    inner_ref[0:2] = own_ref[2:4]
    inner_ref[2:4] = across_ref[2:4]


def pack_across_kernel(across_ref, near_ref, far_ref, packed_ref):
    packed_ref[0:2] = (across_ref[0:2] + far_ref[2:4].astype(f32)).astype(bf16)
    packed_ref[2:4] = (across_ref[2:4] + near_ref[2:4].astype(f32)).astype(bf16)


def first_kernel(
    top, span_x, span_y, position, seeds_hbm, coef_hbm, codes_hbm, h_hbm, cot_hbm,
    rows_out, slots_out, coded, start_ref, term_ref, cot_t_ref, adjoint_ref, rounded_ref, *rest,
):
    sent_refs, (seeds_ref, coef, codes, h_ref, cot_ref, small_sem, h_sem, cot_sem) = rest[:-8], rest[-8:]
    gx, gy = position[0], position[1]
    odd = lax.rem(gx, 2)
    rows = (odd, 1 - odd)
    listed, width = h_ref.shape[1:3]
    small = [
        pltpu.make_async_copy(source, target, small_sem.at[at])
        for at, (source, target) in enumerate(((seeds_hbm, seeds_ref), (codes_hbm, codes), (coef_hbm, coef)))
    ]
    cot_copies, h_copies = [], []
    for at in range(4):
        source = (rows[at // 2], at % 2)
        cot_copies.append(pltpu.make_async_copy(cot_hbm.at[source], cot_ref.at[at], cot_sem.at[at]))
        h_copies.append(pltpu.make_async_copy(h_hbm.at[source], h_ref.at[at], h_sem.at[at]))
    for copy in small + cot_copies + h_copies:
        copy.start()
    coded[...] = jnp.zeros_like(coded)
    for copy in small:
        copy.wait()
    for slot in range(16):
        local = jnp.where(odd == 0, slot // 4 - 1, 2 - slot // 4)
        place_x = lax.rem(gx * 2 + local + span_x, span_x)
        place_y = lax.rem(gy * 2 + slot % 4, span_y)
        start_ref[slot] = start_signs((place_x * span_y + place_y) * width, seeds_ref[...], width)
    places = []
    for at in range(4):
        for k in range(listed):
            code = codes[rows[at // 2], at % 2, k]
            step_x = jnp.where(code >= 6, 1, jnp.where(code >= 3, 0, -1))
            step_y = code - 3 * step_x - 4
            step_x = (1 - 2 * odd) * step_x
            places.append(3 * step_x + step_y + 4)
            slots_out[at * listed + k] = (1 + at // 2 + step_x) * 4 + lax.rem(at % 2 + step_y + 4, 4)
    for at in range(2):
        rows_out[at] = rows[at]
    for copy in cot_copies:
        copy.wait()
    fields = []
    for at in range(4):
        cot = cot_ref[at].astype(f32)
        cot_t = jnp.transpose(cot)
        cot_t_ref[at] = cot_t.astype(bf16)
        adjoint_ref[at] = (coef[top] * cot).astype(bf16)
        fields.append((coef[top] * cot_t).astype(bf16))
    for copy in h_copies:
        copy.wait()
    for at in range(4):
        for k in range(listed):
            coded[at, places[at * listed + k]] = h_ref[at, k]
    push(coded, fields, *sent_refs)
    for at in range(4):
        value = window_product(at, coded, [start_ref.at[pl.ds(4 * row, 4)] for row in range(4)])
        term_ref[at] = value
        rounded_ref[at] = value.astype(bf16)


def forward_kernel(index, has_term, coef, coded, far, outer, inner, near, before_ref, sums_ref, density_ref, rounded_ref, *term_ref):
    for at in range(4):
        before = (before_ref[OWN[at]] if index == 2 else before_ref[at]).astype(f32)
        value = 2.0 * window_product(at, coded, (far, outer, inner, near)) - before
        sums = coef[0] * before + coef[1] * sums_ref[at] if index == 2 else sums_ref[at]
        rounded_ref[at] = value.astype(bf16)
        density_ref[at] = sums + coef[index] * value
        if has_term:
            term_ref[0][at] = value


def adjoint_value(at, index, coef, cot_t_ref, own_ref, across_ref, near_ref, far_ref):
    came = (far_ref if at < 2 else near_ref)[at % 2]
    carried = own_ref[at] + across_ref[at].astype(f32) + came.astype(f32)
    return coef[index] * cot_t_ref[at].astype(f32) + 2.0 * carried


def adjoint_kernel(index, top, coef, coded, *refs):
    arrived, rounded_ref, sent_refs, value_refs = refs[:5], refs[5], refs[6:10], refs[10:]
    fields = []
    for at in range(4):
        value = adjoint_value(at, index, coef, *arrived)
        if index + 2 == top:
            value = value - coef[top] * arrived[0][at].astype(f32)
        for ref in value_refs:
            ref[at] = value
        fields.append(value.astype(bf16))
        rounded_ref[at] = fields[-1]
    push(coded, fields, *sent_refs)


def block_gradients(slots, at, left, windows, listed, store):
    for k in range(listed):
        slot = slots[at * listed + k]
        right = jnp.concatenate([window[slot] for window in windows], axis=1)
        store(k, lax.dot_general(left, right, (((1,), (1,)), ((), ())), preferred_element_type=f32))


def middle_gradient_kernel(parts, slots, *refs):
    count = len(parts)
    adjoints, (sums_ref, windows) = refs[:count], refs[-2:]
    listed = sums_ref.shape[1]
    first = count
    for t in range(count):
        fill_window(refs[first : first + parts[t]], windows.at[t])
        first += parts[t]
    for at in range(4):
        left = [jnp.transpose(2.0 * a[at].astype(f32)).astype(bf16) for a in adjoints]

        def store(k, total, at=at):
            sums_ref[at, k] = total

        block_gradients(slots, at, jnp.concatenate(left, axis=1), [windows.at[t] for t in range(count)], listed, store)


def first_gradient_kernel(slots, coef, older_ref, start_ref, before_ref, *refs):
    arrived, sums_ref = refs[:-1], refs[-1]
    listed = sums_ref.shape[1]
    for at in range(4):
        value = adjoint_value(at, 1, coef, *arrived) - older_ref[at]

        def store(k, total, at=at):
            sums_ref[at, k] = before_ref[at, k] + total

        block_gradients(slots, at, jnp.transpose(value).astype(bf16), (start_ref,), listed, store)


def last_kernel(index, scale, rows, slots, coef, coded, *refs):
    before_ref, sums_ref, adjoint_ref, early_ref, density_hbm, grad_hbm, density, grad, window, density_sem, grad_sem = refs[4:]
    fill_window(refs[:4], window)
    listed = early_ref.shape[1]
    copies = []
    for at in range(4):
        place = (rows[at // 2], at % 2)
        value = 2.0 * window_product(at, coded, refs[:4]) - before_ref[at]
        density[at] = sums_ref[at] + coef[index] * value
        copies.append(pltpu.make_async_copy(density.at[at], density_hbm.at[place], density_sem.at[at]))
        copies[-1].start()

        def store(k, total, at=at):
            grad[at, k] = ((early_ref[at, k] + total) * scale).astype(bf16)

        block_gradients(slots, at, adjoint_ref[at] * bf16(2.0), (window,), listed, store)
        copies.append(pltpu.make_async_copy(grad.at[at], grad_hbm.at[place], grad_sem.at[at]))
        copies[-1].start()
    for copy in copies:
        copy.wait()


def pair_shards(hamiltonian, neighbours, probe_seeds, coefficients, cotangent):
    rows_x, rows_y, listed, width = hamiltonian.shape[:4]
    probes = cotangent.shape[3]
    terms = coefficients.shape[0]
    top = terms - 1
    blocks = rows_x * rows_y
    span_x = rows_x * lax.axis_size("gx")
    span_y = rows_y * lax.axis_size("gy")
    vmem = pl.BlockSpec(memory_space=pltpu.VMEM)
    smem = pl.BlockSpec(memory_space=pltpu.SMEM)
    hbm = pl.BlockSpec(memory_space=pltpu.HBM)

    def field(count, dtype):
        return jax.ShapeDtypeStruct((count, width, probes), dtype)

    def turned(count, dtype):
        return jax.ShapeDtypeStruct((count, probes, width), dtype)

    apply_flops = 2 * blocks * listed * width * width * probes
    sent_shapes = [turned(4, bf16), turned(4, f32), turned(4, f32), turned(4, bf16)]
    window_scratch = pltpu.VMEM((16, width, probes), bf16)

    def kept(values):
        return tuple(pltpu.with_memory_space_constraint(value, pltpu.VMEM) for value in values)

    def call(name, kernel, scalars, operands, out_shape, scratch=(), flops=apply_flops, out_specs=None, in_specs=None):
        return pl.pallas_call(
            kernel,
            in_specs=[smem] * len(scalars) + (in_specs or [vmem] * len(operands)),
            out_specs=out_specs or [vmem] * len(out_shape),
            out_shape=out_shape,
            scratch_shapes=list(scratch),
            compiler_params=pltpu.CompilerParams(vmem_limit_bytes=VMEM_BYTES),
            cost_estimate=pl.CostEstimate(flops=flops, bytes_accessed=1024 * 1024, transcendentals=0),
            name=name,
        )(*scalars, *operands)

    gradient_sums = jax.ShapeDtypeStruct((blocks, listed, width, width), f32)
    shapes = [jax.ShapeDtypeStruct((2,), jnp.int32), jax.ShapeDtypeStruct((blocks * listed,), jnp.int32)]
    shapes += [jax.ShapeDtypeStruct((blocks, 9, width, width), bf16), field(16, bf16), field(4, f32)]
    shapes += [turned(4, bf16), field(4, bf16), field(4, bf16)] + sent_shapes
    rows, slots, coded, start, term, cot_t, adjoint, rounded, to_near, own, to_across, to_far = call(
        "first",
        functools.partial(first_kernel, top, span_x, span_y),
        (jnp.stack([lax.axis_index("gx"), lax.axis_index("gy")]).astype(jnp.int32),),
        tuple(
            pltpu.with_memory_space_constraint(value, pltpu.HBM)
            for value in (probe_seeds.reshape(1, probes), coefficients, neighbours, hamiltonian, cotangent)
        ),
        shapes,
        out_specs=[smem] * 2 + [vmem] * (len(shapes) - 2),
        scratch=(
            pltpu.VMEM((1, probes), jnp.int32),
            pltpu.SMEM(coefficients.shape, f32),
            pltpu.SMEM(neighbours.shape, jnp.int32),
            pltpu.VMEM((blocks, listed, width, width), bf16),
            pltpu.VMEM((blocks, width, probes), bf16),
            pltpu.SemaphoreType.DMA((3,)),
            pltpu.SemaphoreType.DMA((4,)),
            pltpu.SemaphoreType.DMA((4,)),
        ),
        flops=2 * apply_flops,
        in_specs=[hbm] * 5,
    )
    (coded,) = kept((coded,))
    adjoints = {top: adjoint}
    windows = []
    before, sums = start, term
    for index in range(2, terms):
        at = terms - index
        outer, inner = call(
            "pack_rows", pack_rows_kernel, (), kept((rounded, swap_y(rounded))), [field(4, bf16)] * 2, flops=0
        )
        near = swap_near(inner)
        window = kept((swap_far(outer), outer, inner, near))
        from_near, from_far = swap_near(to_near), swap_far(to_far)
        if index == top:
            middle = call(
                "middle_gradient",
                functools.partial(middle_gradient_kernel, (4,) * len(windows)),
                (slots,),
                kept(tuple(adjoints[t] for t in range(2, top)) + tuple(part for shown in windows for part in shown)),
                [gradient_sums],
                scratch=(pltpu.VMEM((terms - 3, 16, width, probes), bf16),),
                flops=(terms - 3) * apply_flops,
            )[0]
            from_near, middle = lax.optimization_barrier((from_near, middle))
        (to_across,) = call(
            "pack_across", pack_across_kernel, (), kept((to_across, from_near, from_far)), [turned(4, bf16)], flops=0
        )
        arrived = kept((cot_t, own, swap_y(to_across), from_near, from_far))
        if index == top:
            break
        windows.append(window)
        has_term = index + 2 <= top
        density, rounded, *following = call(
            "forward",
            functools.partial(forward_kernel, index, has_term),
            (coefficients,), (coded,) + window + kept((before, sums)),
            [field(4, f32), field(4, bf16)] + [field(4, f32)] * has_term,
        )
        before, sums = term, density
        term = following[0] if has_term else None
        has_value = at == 3
        adjoints[at], to_near, own, to_across, to_far, *rest = call(
            "adjoint",
            functools.partial(adjoint_kernel, at, top),
            (coefficients,), (coded,) + arrived,
            [turned(4, bf16)] + sent_shapes + [turned(4, f32)] * has_value,
        )
        if has_value:
            older = rest[0]
    early = call(
        "first_gradient",
        first_gradient_kernel,
        (slots, coefficients), kept((older, start, middle)) + arrived,
        [gradient_sums],
    )[0]
    density, gradient = call(
        "last",
        functools.partial(last_kernel, top, 1.0 / probes),
        (rows, slots, coefficients), (coded,) + window + kept((before, sums, adjoints[top], early)),
        [
            jax.ShapeDtypeStruct(cotangent.shape, f32),
            jax.ShapeDtypeStruct(hamiltonian.shape, bf16),
        ],
        scratch=(
            pltpu.VMEM((4, width, probes), f32),
            pltpu.VMEM((blocks, listed, width, width), bf16),
            window_scratch,
            pltpu.SemaphoreType.DMA((4,)),
            pltpu.SemaphoreType.DMA((4,)),
        ),
        flops=2 * apply_flops,
        out_specs=[hbm, hbm],
    )
    return density, gradient


def shards(hamiltonian, neighbours, probe_seeds, coefficients, cotangent):
    paired = (
        hamiltonian.shape[:2] == (2, 2)
        and lax.axis_size("gy") == 2
        and lax.axis_size("gx") % 2 == 0
        and hamiltonian.shape[2] % 2 == 0
        and coefficients.shape[0] == 5
    )
    run = pair_shards if paired else any_shards
    return run(hamiltonian, neighbours, probe_seeds, coefficients, cotangent)


def solution(mesh):
    placed = (
        P("gx", "gy", None, None, None),
        P("gx", "gy", None),
        P(),
        P(),
        P("gx", "gy", None, None),
    )
    return jax.shard_map(
        shards,
        mesh=mesh,
        in_specs=placed,
        out_specs=(P("gx", "gy", None, None), P("gx", "gy", None, None, None)),
        check_vma=False,
    )
```

```python
import functools

import jax
import jax.numpy as jnp
from jax import lax
from jax.experimental import pallas as pl
from jax.experimental.pallas import tpu as pltpu
from jax.sharding import PartitionSpec as P

offset_table = tuple(((offset_code // 3 - 1, offset_code % 3 - 1) for offset_code in range(9)))


def shifted(value, axis, steps):
    count = lax.axis_size(axis)
    pairs = [(source, (source + steps) % count) for source in range(count)]
    return lax.ppermute(value, axis, pairs)


def padded_2(block, sides, width):
    for axis, dim in sides:
        count = lax.axis_size(axis)
        forward = [(i, i + 1) for i in range(count - 1)]
        forward.append((count - 1, 0))
        backward = [(target, source) for source, target in forward]
        low = lax.ppermute(
            lax.slice_in_dim(block, block.shape[dim] - width, None, axis=dim), axis, forward
        )
        high = lax.ppermute(lax.slice_in_dim(block, 0, width, axis=dim), axis, backward)
        block = jnp.concatenate([low, block, high], axis=dim)
    return block


def probe_signs(global_rows, seed_values):
    hashed = global_rows[..., None] * jnp.int32(-1640531535)
    hashed = hashed ^ seed_values
    hashed = hashed ^ hashed >> 15
    hashed = hashed * jnp.int32(739982445)
    hashed = hashed ^ hashed >> 12
    parity = hashed >> 7 & 1
    return (1 - 2 * parity).astype(jnp.float32)


def by_offset(hamiltonian, neighbours):
    onehot = (neighbours[..., None] == jnp.arange(9, dtype=jnp.int32)).astype(jnp.bfloat16)
    picked = jnp.einsum(
        "abkc,abkxy->abcxy", onehot, hamiltonian, preferred_element_type=jnp.float32
    )
    return picked.astype(jnp.bfloat16)


def forward_apply(selected, padded):
    rows_x, rows_y = (selected.shape[0], selected.shape[1])
    summed = jnp.zeros((rows_x, rows_y, selected.shape[3], padded.shape[3]), jnp.float32)
    for offset_code, (step_x, step_y) in enumerate(offset_table):
        window = padded[1 + step_x : 1 + step_x + rows_x, 1 + step_y : 1 + step_y + rows_y]
        summed = summed + jnp.einsum(
            "abxy,abyp->abxp",
            selected[:, :, offset_code],
            window,
            preferred_element_type=jnp.float32,
        )
    return summed


def push_transpose(selected, adjoint_bf16):
    rows_x, rows_y = (selected.shape[0], selected.shape[1])
    gathered = jnp.zeros((rows_x + 2, rows_y + 2) + adjoint_bf16.shape[2:], jnp.float32)
    for offset_code, (step_x, step_y) in enumerate(offset_table):
        product = jnp.einsum(
            "abyx,abyp->abxp",
            selected[:, :, offset_code],
            adjoint_bf16,
            preferred_element_type=jnp.float32,
        )
        gathered = gathered + jnp.pad(
            product, ((1 + step_x, 1 - step_x), (1 + step_y, 1 - step_y), (0, 0), (0, 0))
        )
    for offset_by, source, target in ((-1, 0, rows_x), (1, rows_x + 1, 1)):
        moved = shifted(gathered[source], "gx", offset_by)
        gathered = gathered.at[target].add(moved)
    middle = gathered[1 : rows_x + 1]
    for offset_by, source, target in ((-1, 0, rows_y), (1, rows_y + 1, 1)):
        moved = shifted(middle[:, source], "gy", offset_by)
        middle = middle.at[:, target].add(moved)
    return middle[:, 1 : rows_y + 1]


def any_shards(hamiltonian, neighbours, probe_seeds, coefficients, cotangent):
    rows_x, rows_y = (hamiltonian.shape[0], hamiltonian.shape[1])
    width = hamiltonian.shape[3]
    probes = cotangent.shape[3]
    count_terms = coefficients.shape[0]
    span_x = rows_x * lax.axis_size("gx")
    span_y = rows_y * lax.axis_size("gy")
    place_x = (lax.axis_index("gx") * rows_x + jnp.arange(rows_x + 2, dtype=jnp.int32) - 1) % span_x
    place_y = (lax.axis_index("gy") * rows_y + jnp.arange(rows_y + 2, dtype=jnp.int32) - 1) % span_y
    orbital = jnp.arange(width, dtype=jnp.int32)
    global_rows = (place_x[:, None] * span_y + place_y[None, :])[:, :, None] * width + orbital[
        None, None, :
    ]
    start_padded = probe_signs(global_rows, probe_seeds)
    start_term = start_padded[1 : rows_x + 1, 1 : rows_y + 1]
    selected = by_offset(hamiltonian, neighbours)
    term_pads = [start_padded.astype(jnp.bfloat16)]
    previous = start_term
    current = forward_apply(selected, term_pads[0])
    density = coefficients[0] * start_term + coefficients[1] * current
    for index in range(2, count_terms):
        padded = padded_2(current.astype(jnp.bfloat16), (("gx", 0), ("gy", 1)), 1)
        term_pads.append(padded)
        following = 2.0 * forward_apply(selected, padded) - previous
        previous, current = (current, following)
        density = density + coefficients[index] * current
    seed_field = cotangent.astype(jnp.float32)
    adjoints = {}
    adjoint_rounded = {}
    for index in range(count_terms - 1, 0, -1):
        value = coefficients[index] * seed_field
        if index + 1 < count_terms:
            carried = push_transpose(selected, adjoint_rounded[index + 1])
            value = value + 2.0 * carried
        if index + 2 < count_terms:
            value = value - adjoints[index + 2]
        adjoints[index] = value
        adjoint_rounded[index] = value.astype(jnp.bfloat16)
    adjoint_stack = jnp.concatenate(
        [adjoint_rounded[index] * (1.0 if index == 1 else 2.0) for index in range(1, count_terms)],
        axis=3,
    )
    term_stack = jnp.concatenate(term_pads, axis=3)
    gradient = jnp.zeros(hamiltonian.shape, jnp.float32)
    for offset_code, (step_x, step_y) in enumerate(offset_table):
        window = term_stack[1 + step_x : 1 + step_x + rows_x, 1 + step_y : 1 + step_y + rows_y]
        block_grad = jnp.einsum(
            "abxq,abyq->abxy", adjoint_stack, window, preferred_element_type=jnp.float32
        )
        gradient = gradient + jnp.where(
            (neighbours == offset_code)[..., None, None], block_grad[:, :, None], 0.0
        )
    return (density, (gradient * (1.0 / probes)).astype(jnp.bfloat16))


bf16 = jnp.bfloat16
f32 = jnp.float32
VMEM_BYTES = 16 * 1024 * 1024
OWN = (4, 5, 8, 9)


def swap_y(value):
    return lax.ppermute(value, "gy", [(0, 1), (1, 0)])


def swap_near(value):
    count = lax.axis_size("gx")
    return lax.ppermute(value, "gx", [(i, i ^ 1) for i in range(count)])


def swap_far(value):
    count = lax.axis_size("gx")
    pairs = [(i, (i + 1) % count if i % 2 else (i - 1) % count) for i in range(count)]
    return lax.ppermute(value, "gx", pairs)


def start_signs(rows_from, seeds, width):
    shape = (width, seeds.shape[1])
    hashed = (rows_from + lax.broadcasted_iota(jnp.int32, shape, 0)) * jnp.int32(-1640531535)
    hashed = hashed ^ seeds
    hashed = hashed ^ hashed >> 15
    hashed = hashed * jnp.int32(739982445)
    hashed = hashed ^ hashed >> 12
    return jnp.where((hashed & 128) == 0, f32(1.0), f32(-1.0)).astype(bf16)


def step_of(code):
    return code // 3 - 1, code % 3 - 1


def window_product(at, coded, rows_of_blocks):
    right = []
    for code in range(9):
        step_x, step_y = step_of(code)
        right.append(rows_of_blocks[1 + at // 2 + step_x][(at % 2 + step_y) % 4])
    left = jnp.concatenate([coded[at, code] for code in range(9)], axis=1)
    return jnp.dot(left, jnp.concatenate(right, axis=0), preferred_element_type=f32)


def push(coded, fields, near_ref, own_ref, across_ref, far_ref):
    for col in range(4):
        sources = [(b, (col - b + 1) % 4 - 1) for b in range(2) if (col - b + 1) % 4 < 3]

        def blocks(row, *steps):
            return [
                jnp.concatenate([coded[2 * row + b, 3 * (step_x + 1) + step_y + 1] for step_x in steps], axis=1)
                for b, step_y in sources
            ]

        def total(rows, right):
            left = jnp.concatenate([fields[2 * row + b] for row in rows for b, _ in sources], axis=1)
            return jnp.dot(left, jnp.concatenate(right, axis=0), preferred_element_type=f32)

        far_ref[col] = total((0,), blocks(0, -1)).astype(bf16)
        near_ref[col] = total((1,), blocks(1, 1)).astype(bf16)
        middle = total((0, 1), blocks(0, 0, 1) + blocks(1, -1, 0))
        width = middle.shape[1] // 2
        ref = own_ref if col < 2 else across_ref
        ref[col % 2] = middle[:, :width]
        ref[2 + col % 2] = middle[:, width:]


def fill_window(parts, window):
    first = 0
    for part in parts:
        window[first : first + part.shape[0]] = part[...]
        first += part.shape[0]


def pack_rows_kernel(own_ref, across_ref, outer_ref, inner_ref):
    outer_ref[0:2] = own_ref[0:2]
    outer_ref[2:4] = across_ref[0:2]
    inner_ref[0:2] = own_ref[2:4]
    inner_ref[2:4] = across_ref[2:4]


def pack_across_kernel(across_ref, near_ref, far_ref, packed_ref):
    packed_ref[0:2] = (across_ref[0:2] + far_ref[2:4].astype(f32)).astype(bf16)
    packed_ref[2:4] = (across_ref[2:4] + near_ref[2:4].astype(f32)).astype(bf16)


def first_kernel(
    top, span_x, span_y, seeds_hbm, coef_hbm, codes_hbm, h_hbm, cot_hbm,
    rows_out, slots_out, coded, start_ref, term_ref, cot_t_ref, adjoint_ref, rounded_ref, *rest,
):
    sent_refs, (seeds_ref, coef, codes, h_ref, cot_ref, small_sem, h_sem, cot_sem) = rest[:-8], rest[-8:]
    gx, gy = lax.axis_index("gx"), lax.axis_index("gy")
    odd = lax.rem(gx, 2)
    rows = (odd, 1 - odd)
    listed, width = h_ref.shape[1:3]
    small = [
        pltpu.make_async_copy(source, target, small_sem.at[at])
        for at, (source, target) in enumerate(((seeds_hbm, seeds_ref), (codes_hbm, codes), (coef_hbm, coef)))
    ]
    cot_copies, h_copies = [], []
    for at in range(4):
        source = (rows[at // 2], at % 2)
        cot_copies.append(pltpu.make_async_copy(cot_hbm.at[source], cot_ref.at[at], cot_sem.at[at]))
        h_copies.append(pltpu.make_async_copy(h_hbm.at[source], h_ref.at[at], h_sem.at[at]))
    for copy in small + cot_copies + h_copies:
        copy.start()
    coded[...] = jnp.zeros_like(coded)
    for copy in small:
        copy.wait()
    for slot in range(16):
        local = jnp.where(odd == 0, slot // 4 - 1, 2 - slot // 4)
        place_x = lax.rem(gx * 2 + local + span_x, span_x)
        place_y = lax.rem(gy * 2 + slot % 4, span_y)
        start_ref[slot] = start_signs((place_x * span_y + place_y) * width, seeds_ref[...], width)
    places = []
    for at in range(4):
        for k in range(listed):
            code = codes[rows[at // 2], at % 2, k]
            step_x = jnp.where(code >= 6, 1, jnp.where(code >= 3, 0, -1))
            step_y = code - 3 * step_x - 4
            step_x = (1 - 2 * odd) * step_x
            places.append(3 * step_x + step_y + 4)
            slots_out[at * listed + k] = (1 + at // 2 + step_x) * 4 + lax.rem(at % 2 + step_y + 4, 4)
    for at in range(2):
        rows_out[at] = rows[at]
    for copy in cot_copies:
        copy.wait()
    fields = []
    for at in range(4):
        cot = cot_ref[at].astype(f32)
        cot_t = jnp.transpose(cot)
        cot_t_ref[at] = cot_t.astype(bf16)
        adjoint_ref[at] = (coef[top] * cot).astype(bf16)
        fields.append((coef[top] * cot_t).astype(bf16))
    for at in range(4):
        h_copies[at].wait()
        for k in range(listed):
            coded[at, places[at * listed + k]] = h_ref[at, k]
    push(coded, fields, *sent_refs)
    for at in range(4):
        value = window_product(at, coded, [start_ref.at[pl.ds(4 * row, 4)] for row in range(4)])
        term_ref[at] = value
        rounded_ref[at] = value.astype(bf16)


def forward_kernel(index, has_term, coef, coded, far, outer, inner, near, before_ref, sums_ref, density_ref, rounded_ref, *term_ref):
    for at in range(4):
        before = (before_ref[OWN[at]] if index == 2 else before_ref[at]).astype(f32)
        value = 2.0 * window_product(at, coded, (far, outer, inner, near)) - before
        sums = coef[0] * before + coef[1] * sums_ref[at] if index == 2 else sums_ref[at]
        rounded_ref[at] = value.astype(bf16)
        density_ref[at] = sums + coef[index] * value
        if has_term:
            term_ref[0][at] = value


def adjoint_value(at, index, coef, cot_t_ref, own_ref, across_ref, near_ref, far_ref):
    came = (far_ref if at < 2 else near_ref)[at % 2]
    carried = own_ref[at] + across_ref[at].astype(f32) + came.astype(f32)
    return coef[index] * cot_t_ref[at].astype(f32) + 2.0 * carried


def adjoint_kernel(index, top, coef, coded, *refs):
    arrived, rounded_ref, sent_refs, value_refs = refs[:5], refs[5], refs[6:10], refs[10:]
    fields = []
    for at in range(4):
        value = adjoint_value(at, index, coef, *arrived)
        if index + 2 == top:
            value = value - coef[top] * arrived[0][at].astype(f32)
        for ref in value_refs:
            ref[at] = value
        fields.append(value.astype(bf16))
        rounded_ref[at] = fields[-1]
    push(coded, fields, *sent_refs)


def block_gradients(slots, at, left, windows, listed, store):
    for k in range(listed):
        slot = slots[at * listed + k]
        right = jnp.concatenate([window[slot] for window in windows], axis=1)
        store(k, lax.dot_general(left, right, (((1,), (1,)), ((), ())), preferred_element_type=f32))


def middle_gradient_kernel(parts, slots, *refs):
    count = len(parts)
    adjoints, (sums_ref, windows) = refs[:count], refs[-2:]
    listed = sums_ref.shape[1]
    first = count
    for t in range(count):
        fill_window(refs[first : first + parts[t]], windows.at[t])
        first += parts[t]
    for at in range(4):
        left = [jnp.transpose(2.0 * a[at].astype(f32)).astype(bf16) for a in adjoints]

        def store(k, total, at=at):
            sums_ref[at, k] = total

        block_gradients(slots, at, jnp.concatenate(left, axis=1), [windows.at[t] for t in range(count)], listed, store)


def first_gradient_kernel(scale, slots, coef, older_ref, start_ref, before_ref, *refs):
    arrived, sums_ref = refs[:-1], refs[-1]
    listed = sums_ref.shape[1]
    for at in range(4):
        value = adjoint_value(at, 1, coef, *arrived) - older_ref[at]

        def store(k, total, at=at):
            sums_ref[at, k] = (before_ref[at, k] + total) * scale

        block_gradients(slots, at, jnp.transpose(value).astype(bf16), (start_ref,), listed, store)


def last_kernel(index, scale, rows, slots, coef, coded, *refs):
    before_ref, sums_ref, adjoint_ref, early_ref, density_hbm, grad_hbm, density, grad, window, density_sem, grad_sem = refs[4:]
    fill_window(refs[:4], window)
    listed = early_ref.shape[1]
    copies = []
    for at in range(4):
        place = (rows[at // 2], at % 2)
        value = 2.0 * window_product(at, coded, refs[:4]) - before_ref[at]
        density[at] = sums_ref[at] + coef[index] * value
        copies.append(pltpu.make_async_copy(density.at[at], density_hbm.at[place], density_sem.at[at]))
        copies[-1].start()

        def store(k, total, at=at):
            grad[at, k] = (early_ref[at, k] + total).astype(bf16)

        block_gradients(slots, at, adjoint_ref[at] * bf16(2.0 * scale), (window,), listed, store)
        copies.append(pltpu.make_async_copy(grad.at[at], grad_hbm.at[place], grad_sem.at[at]))
        copies[-1].start()
    for copy in copies:
        copy.wait()


def pair_shards(hamiltonian, neighbours, probe_seeds, coefficients, cotangent):
    rows_x, rows_y, listed, width = hamiltonian.shape[:4]
    probes = cotangent.shape[3]
    terms = coefficients.shape[0]
    top = terms - 1
    blocks = rows_x * rows_y
    span_x = rows_x * lax.axis_size("gx")
    span_y = rows_y * lax.axis_size("gy")
    vmem = pl.BlockSpec(memory_space=pltpu.VMEM)
    smem = pl.BlockSpec(memory_space=pltpu.SMEM)
    hbm = pl.BlockSpec(memory_space=pltpu.HBM)

    def field(count, dtype):
        return jax.ShapeDtypeStruct((count, width, probes), dtype)

    def turned(count, dtype):
        return jax.ShapeDtypeStruct((count, probes, width), dtype)

    apply_flops = 2 * blocks * listed * width * width * probes
    sent_shapes = [turned(4, bf16), turned(4, f32), turned(4, f32), turned(4, bf16)]
    window_scratch = pltpu.VMEM((16, width, probes), bf16)

    def kept(values):
        return tuple(pltpu.with_memory_space_constraint(value, pltpu.VMEM) for value in values)

    def call(name, kernel, scalars, operands, out_shape, scratch=(), flops=apply_flops, out_specs=None, in_specs=None):
        return pl.pallas_call(
            kernel,
            in_specs=[smem] * len(scalars) + (in_specs or [vmem] * len(operands)),
            out_specs=out_specs or [vmem] * len(out_shape),
            out_shape=out_shape,
            scratch_shapes=list(scratch),
            compiler_params=pltpu.CompilerParams(vmem_limit_bytes=VMEM_BYTES),
            cost_estimate=pl.CostEstimate(flops=flops, bytes_accessed=1024 * 1024, transcendentals=0),
            name=name,
        )(*scalars, *operands)

    gradient_sums = jax.ShapeDtypeStruct((blocks, listed, width, width), f32)
    shapes = [jax.ShapeDtypeStruct((2,), jnp.int32), jax.ShapeDtypeStruct((blocks * listed,), jnp.int32)]
    shapes += [jax.ShapeDtypeStruct((blocks, 9, width, width), bf16), field(16, bf16), field(4, f32)]
    shapes += [turned(4, bf16), field(4, bf16), field(4, bf16)] + sent_shapes
    rows, slots, coded, start, term, cot_t, adjoint, rounded, to_near, own, to_across, to_far = call(
        "first",
        functools.partial(first_kernel, top, span_x, span_y),
        (),
        tuple(
            pltpu.with_memory_space_constraint(value, pltpu.HBM)
            for value in (probe_seeds.reshape(1, probes), coefficients, neighbours, hamiltonian, cotangent)
        ),
        shapes,
        out_specs=[smem] * 2 + [vmem] * (len(shapes) - 2),
        scratch=(
            pltpu.VMEM((1, probes), jnp.int32),
            pltpu.SMEM(coefficients.shape, f32),
            pltpu.SMEM(neighbours.shape, jnp.int32),
            pltpu.VMEM((blocks, listed, width, width), bf16),
            pltpu.VMEM((blocks, width, probes), bf16),
            pltpu.SemaphoreType.DMA((3,)),
            pltpu.SemaphoreType.DMA((4,)),
            pltpu.SemaphoreType.DMA((4,)),
        ),
        flops=2 * apply_flops,
        in_specs=[hbm] * 5,
    )
    (coded,) = kept((coded,))
    adjoints = {top: adjoint}
    windows = []
    before, sums = start, term
    for index in range(2, terms):
        at = terms - index
        outer, inner = call(
            "pack_rows", pack_rows_kernel, (), kept((rounded, swap_y(rounded))), [field(4, bf16)] * 2, flops=0
        )
        near = swap_near(inner)
        window = kept((swap_far(outer), outer, inner, near))
        from_near, from_far = swap_near(to_near), swap_far(to_far)
        if index == top:
            middle = call(
                "middle_gradient",
                functools.partial(middle_gradient_kernel, (4,) * len(windows)),
                (slots,),
                kept(tuple(adjoints[t] for t in range(2, top)) + tuple(part for shown in windows for part in shown)),
                [gradient_sums],
                scratch=(pltpu.VMEM((terms - 3, 16, width, probes), bf16),),
                flops=(terms - 3) * apply_flops,
            )[0]
            from_near, middle = lax.optimization_barrier((from_near, middle))
        (to_across,) = call(
            "pack_across", pack_across_kernel, (), kept((to_across, from_near, from_far)), [turned(4, bf16)], flops=0
        )
        arrived = kept((cot_t, own, swap_y(to_across), from_near, from_far))
        if index == top:
            break
        windows.append(window)
        has_term = index + 2 <= top
        density, rounded, *following = call(
            "forward",
            functools.partial(forward_kernel, index, has_term),
            (coefficients,), (coded,) + window + kept((before, sums)),
            [field(4, f32), field(4, bf16)] + [field(4, f32)] * has_term,
        )
        before, sums = term, density
        term = following[0] if has_term else None
        has_value = at == 3
        adjoints[at], to_near, own, to_across, to_far, *rest = call(
            "adjoint",
            functools.partial(adjoint_kernel, at, top),
            (coefficients,), (coded,) + arrived,
            [turned(4, bf16)] + sent_shapes + [turned(4, f32)] * has_value,
        )
        if has_value:
            older = rest[0]
    early = call(
        "first_gradient",
        functools.partial(first_gradient_kernel, 1.0 / probes),
        (slots, coefficients), kept((older, start, middle)) + arrived,
        [gradient_sums],
    )[0]
    density, gradient = call(
        "last",
        functools.partial(last_kernel, top, 1.0 / probes),
        (rows, slots, coefficients), (coded,) + window + kept((before, sums, adjoints[top], early)),
        [
            jax.ShapeDtypeStruct(cotangent.shape, f32),
            jax.ShapeDtypeStruct(hamiltonian.shape, bf16),
        ],
        scratch=(
            pltpu.VMEM((4, width, probes), f32),
            pltpu.VMEM((blocks, listed, width, width), bf16),
            window_scratch,
            pltpu.SemaphoreType.DMA((4,)),
            pltpu.SemaphoreType.DMA((4,)),
        ),
        flops=2 * apply_flops,
        out_specs=[hbm, hbm],
    )
    return density, gradient


def shards(hamiltonian, neighbours, probe_seeds, coefficients, cotangent):
    paired = (
        hamiltonian.shape[:2] == (2, 2)
        and lax.axis_size("gy") == 2
        and lax.axis_size("gx") % 2 == 0
        and hamiltonian.shape[2] % 2 == 0
        and coefficients.shape[0] == 5
    )
    run = pair_shards if paired else any_shards
    return run(hamiltonian, neighbours, probe_seeds, coefficients, cotangent)


def solution(mesh):
    placed = (
        P("gx", "gy", None, None, None),
        P("gx", "gy", None),
        P(),
        P(),
        P("gx", "gy", None, None),
    )
    return jax.shard_map(
        shards,
        mesh=mesh,
        in_specs=placed,
        out_specs=(P("gx", "gy", None, None), P("gx", "gy", None, None, None)),
        check_vma=False,
    )
```

```python
import functools

import jax
import jax.numpy as jnp
from jax import lax
from jax.experimental import pallas as pl
from jax.experimental.pallas import tpu as pltpu
from jax.sharding import PartitionSpec as P

offset_table = tuple(((offset_code // 3 - 1, offset_code % 3 - 1) for offset_code in range(9)))


def shifted(value, axis, steps):
    count = lax.axis_size(axis)
    pairs = [(source, (source + steps) % count) for source in range(count)]
    return lax.ppermute(value, axis, pairs)


def padded_2(block, sides, width):
    for axis, dim in sides:
        count = lax.axis_size(axis)
        forward = [(i, i + 1) for i in range(count - 1)]
        forward.append((count - 1, 0))
        backward = [(target, source) for source, target in forward]
        low = lax.ppermute(
            lax.slice_in_dim(block, block.shape[dim] - width, None, axis=dim), axis, forward
        )
        high = lax.ppermute(lax.slice_in_dim(block, 0, width, axis=dim), axis, backward)
        block = jnp.concatenate([low, block, high], axis=dim)
    return block


def probe_signs(global_rows, seed_values):
    hashed = global_rows[..., None] * jnp.int32(-1640531535)
    hashed = hashed ^ seed_values
    hashed = hashed ^ hashed >> 15
    hashed = hashed * jnp.int32(739982445)
    hashed = hashed ^ hashed >> 12
    parity = hashed >> 7 & 1
    return (1 - 2 * parity).astype(jnp.float32)


def by_offset(hamiltonian, neighbours):
    onehot = (neighbours[..., None] == jnp.arange(9, dtype=jnp.int32)).astype(jnp.bfloat16)
    picked = jnp.einsum(
        "abkc,abkxy->abcxy", onehot, hamiltonian, preferred_element_type=jnp.float32
    )
    return picked.astype(jnp.bfloat16)


def forward_apply(selected, padded):
    rows_x, rows_y = (selected.shape[0], selected.shape[1])
    summed = jnp.zeros((rows_x, rows_y, selected.shape[3], padded.shape[3]), jnp.float32)
    for offset_code, (step_x, step_y) in enumerate(offset_table):
        window = padded[1 + step_x : 1 + step_x + rows_x, 1 + step_y : 1 + step_y + rows_y]
        summed = summed + jnp.einsum(
            "abxy,abyp->abxp",
            selected[:, :, offset_code],
            window,
            preferred_element_type=jnp.float32,
        )
    return summed


def push_transpose(selected, adjoint_bf16):
    rows_x, rows_y = (selected.shape[0], selected.shape[1])
    gathered = jnp.zeros((rows_x + 2, rows_y + 2) + adjoint_bf16.shape[2:], jnp.float32)
    for offset_code, (step_x, step_y) in enumerate(offset_table):
        product = jnp.einsum(
            "abyx,abyp->abxp",
            selected[:, :, offset_code],
            adjoint_bf16,
            preferred_element_type=jnp.float32,
        )
        gathered = gathered + jnp.pad(
            product, ((1 + step_x, 1 - step_x), (1 + step_y, 1 - step_y), (0, 0), (0, 0))
        )
    for offset_by, source, target in ((-1, 0, rows_x), (1, rows_x + 1, 1)):
        moved = shifted(gathered[source], "gx", offset_by)
        gathered = gathered.at[target].add(moved)
    middle = gathered[1 : rows_x + 1]
    for offset_by, source, target in ((-1, 0, rows_y), (1, rows_y + 1, 1)):
        moved = shifted(middle[:, source], "gy", offset_by)
        middle = middle.at[:, target].add(moved)
    return middle[:, 1 : rows_y + 1]


def any_shards(hamiltonian, neighbours, probe_seeds, coefficients, cotangent):
    rows_x, rows_y = (hamiltonian.shape[0], hamiltonian.shape[1])
    width = hamiltonian.shape[3]
    probes = cotangent.shape[3]
    count_terms = coefficients.shape[0]
    span_x = rows_x * lax.axis_size("gx")
    span_y = rows_y * lax.axis_size("gy")
    place_x = (lax.axis_index("gx") * rows_x + jnp.arange(rows_x + 2, dtype=jnp.int32) - 1) % span_x
    place_y = (lax.axis_index("gy") * rows_y + jnp.arange(rows_y + 2, dtype=jnp.int32) - 1) % span_y
    orbital = jnp.arange(width, dtype=jnp.int32)
    global_rows = (place_x[:, None] * span_y + place_y[None, :])[:, :, None] * width + orbital[
        None, None, :
    ]
    start_padded = probe_signs(global_rows, probe_seeds)
    start_term = start_padded[1 : rows_x + 1, 1 : rows_y + 1]
    selected = by_offset(hamiltonian, neighbours)
    term_pads = [start_padded.astype(jnp.bfloat16)]
    previous = start_term
    current = forward_apply(selected, term_pads[0])
    density = coefficients[0] * start_term + coefficients[1] * current
    for index in range(2, count_terms):
        padded = padded_2(current.astype(jnp.bfloat16), (("gx", 0), ("gy", 1)), 1)
        term_pads.append(padded)
        following = 2.0 * forward_apply(selected, padded) - previous
        previous, current = (current, following)
        density = density + coefficients[index] * current
    seed_field = cotangent.astype(jnp.float32)
    adjoints = {}
    adjoint_rounded = {}
    for index in range(count_terms - 1, 0, -1):
        value = coefficients[index] * seed_field
        if index + 1 < count_terms:
            carried = push_transpose(selected, adjoint_rounded[index + 1])
            value = value + 2.0 * carried
        if index + 2 < count_terms:
            value = value - adjoints[index + 2]
        adjoints[index] = value
        adjoint_rounded[index] = value.astype(jnp.bfloat16)
    adjoint_stack = jnp.concatenate(
        [adjoint_rounded[index] * (1.0 if index == 1 else 2.0) for index in range(1, count_terms)],
        axis=3,
    )
    term_stack = jnp.concatenate(term_pads, axis=3)
    gradient = jnp.zeros(hamiltonian.shape, jnp.float32)
    for offset_code, (step_x, step_y) in enumerate(offset_table):
        window = term_stack[1 + step_x : 1 + step_x + rows_x, 1 + step_y : 1 + step_y + rows_y]
        block_grad = jnp.einsum(
            "abxq,abyq->abxy", adjoint_stack, window, preferred_element_type=jnp.float32
        )
        gradient = gradient + jnp.where(
            (neighbours == offset_code)[..., None, None], block_grad[:, :, None], 0.0
        )
    return (density, (gradient * (1.0 / probes)).astype(jnp.bfloat16))


bf16 = jnp.bfloat16
f32 = jnp.float32
VMEM_BYTES = 16 * 1024 * 1024
OWN = (4, 5, 8, 9)


def swap_y(value):
    return lax.ppermute(value, "gy", [(0, 1), (1, 0)])


def swap_near(value):
    count = lax.axis_size("gx")
    return lax.ppermute(value, "gx", [(i, i ^ 1) for i in range(count)])


def swap_far(value):
    count = lax.axis_size("gx")
    pairs = [(i, (i + 1) % count if i % 2 else (i - 1) % count) for i in range(count)]
    return lax.ppermute(value, "gx", pairs)


def start_signs(rows_from, seeds, width):
    hashed = (rows_from + lax.broadcasted_iota(jnp.int32, (width, 1), 0)) * jnp.int32(-1640531535)
    hashed = hashed ^ seeds
    hashed = hashed ^ hashed >> 15
    hashed = hashed * jnp.int32(739982445)
    hashed = hashed ^ hashed >> 12
    return jnp.where((hashed & 128) == 0, f32(1.0), f32(-1.0)).astype(bf16)


def step_of(code):
    return code // 3 - 1, code % 3 - 1


def window_product(at, coded, rows_of_blocks):
    right = []
    for code in range(9):
        step_x, step_y = step_of(code)
        right.append(rows_of_blocks[1 + at // 2 + step_x][(at % 2 + step_y) % 4])
    left = jnp.concatenate([coded[at, code] for code in range(9)], axis=1)
    return jnp.dot(left, jnp.concatenate(right, axis=0), preferred_element_type=f32)


def push(coded, fields, near_ref, own_ref, across_ref, far_ref):
    for col in range(4):
        sources = [(b, (col - b + 1) % 4 - 1) for b in range(2) if (col - b + 1) % 4 < 3]

        def blocks(row, *steps):
            return [
                jnp.concatenate([coded[2 * row + b, 3 * (step_x + 1) + step_y + 1] for step_x in steps], axis=1)
                for b, step_y in sources
            ]

        def total(rows, right):
            left = jnp.concatenate([fields[2 * row + b] for row in rows for b, _ in sources], axis=1)
            return jnp.dot(left, jnp.concatenate(right, axis=0), preferred_element_type=f32)

        far_ref[col] = total((0,), blocks(0, -1)).astype(bf16)
        near_ref[col] = total((1,), blocks(1, 1)).astype(bf16)
        middle = total((0, 1), blocks(0, 0, 1) + blocks(1, -1, 0))
        width = middle.shape[1] // 2
        ref = own_ref if col < 2 else across_ref
        ref[col % 2] = middle[:, :width]
        ref[2 + col % 2] = middle[:, width:]


def fill_window(parts, window):
    first = 0
    for part in parts:
        window[first : first + part.shape[0]] = part[...]
        first += part.shape[0]


def pack_rows_kernel(own_ref, across_ref, outer_ref, inner_ref):
    outer_ref[0:2] = own_ref[0:2]
    outer_ref[2:4] = across_ref[0:2]
    inner_ref[0:2] = own_ref[2:4]
    inner_ref[2:4] = across_ref[2:4]


def pack_across_kernel(across_ref, near_ref, far_ref, packed_ref):
    packed_ref[0:2] = (across_ref[0:2] + far_ref[2:4].astype(f32)).astype(bf16)
    packed_ref[2:4] = (across_ref[2:4] + near_ref[2:4].astype(f32)).astype(bf16)


def first_kernel(
    top, span_x, span_y, seeds_hbm, coef_hbm, codes_hbm, h_hbm, cot_hbm,
    rows_out, slots_out, coded, start_ref, term_ref, cot_t_ref, adjoint_ref, rounded_ref, *rest,
):
    sent_refs, (seeds_ref, coef, codes, h_ref, cot_ref, small_sem, h_sem, cot_sem) = rest[:-8], rest[-8:]
    gx, gy = lax.axis_index("gx"), lax.axis_index("gy")
    odd = lax.rem(gx, 2)
    rows = (odd, 1 - odd)
    listed, width = h_ref.shape[1:3]
    small = [
        pltpu.make_async_copy(source, target, small_sem.at[at])
        for at, (source, target) in enumerate(((seeds_hbm, seeds_ref), (codes_hbm, codes), (coef_hbm, coef)))
    ]
    cot_copies, h_copies = [], []
    for at in range(4):
        source = (rows[at // 2], at % 2)
        cot_copies.append(pltpu.make_async_copy(cot_hbm.at[source], cot_ref.at[at], cot_sem.at[at]))
        h_copies.append(pltpu.make_async_copy(h_hbm.at[source], h_ref.at[at], h_sem.at[at]))
    for copy in small + cot_copies + h_copies:
        copy.start()
    coded[...] = jnp.zeros_like(coded)
    for copy in small:
        copy.wait()
    for slot in range(16):
        local = jnp.where(odd == 0, slot // 4 - 1, 2 - slot // 4)
        place_x = lax.rem(gx * 2 + local + span_x, span_x)
        place_y = lax.rem(gy * 2 + slot % 4, span_y)
        start_ref[slot] = start_signs((place_x * span_y + place_y) * width, seeds_ref[...], width)
    places = []
    for at in range(4):
        for k in range(listed):
            code = codes[rows[at // 2], at % 2, k]
            step_x = jnp.where(code >= 6, 1, jnp.where(code >= 3, 0, -1))
            step_y = code - 3 * step_x - 4
            step_x = (1 - 2 * odd) * step_x
            places.append(3 * step_x + step_y + 4)
            slots_out[at * listed + k] = (1 + at // 2 + step_x) * 4 + lax.rem(at % 2 + step_y + 4, 4)
    for at in range(2):
        rows_out[at] = rows[at]
    for copy in cot_copies:
        copy.wait()
    fields = []
    for at in range(4):
        cot = cot_ref[at].astype(f32)
        cot_t = jnp.transpose(cot)
        cot_t_ref[at] = cot_t.astype(bf16)
        adjoint_ref[at] = (coef[top] * cot).astype(bf16)
        fields.append((coef[top] * cot_t).astype(bf16))
    for at in range(4):
        h_copies[at].wait()
        for k in range(listed):
            coded[at, places[at * listed + k]] = h_ref[at, k]
    push(coded, fields, *sent_refs)
    for at in range(4):
        value = window_product(at, coded, [start_ref.at[pl.ds(4 * row, 4)] for row in range(4)])
        term_ref[at] = value
        rounded_ref[at] = value.astype(bf16)


def forward_kernel(index, has_term, coef, coded, far, outer, inner, near, before_ref, sums_ref, density_ref, rounded_ref, *term_ref):
    for at in range(4):
        before = (before_ref[OWN[at]] if index == 2 else before_ref[at]).astype(f32)
        value = 2.0 * window_product(at, coded, (far, outer, inner, near)) - before
        sums = coef[0] * before + coef[1] * sums_ref[at] if index == 2 else sums_ref[at]
        rounded_ref[at] = value.astype(bf16)
        density_ref[at] = sums + coef[index] * value
        if has_term:
            term_ref[0][at] = value


def adjoint_value(at, index, coef, cot_t_ref, own_ref, across_ref, near_ref, far_ref):
    came = (far_ref if at < 2 else near_ref)[at % 2]
    carried = own_ref[at] + across_ref[at].astype(f32) + came.astype(f32)
    return coef[index] * cot_t_ref[at].astype(f32) + 2.0 * carried


def adjoint_kernel(index, top, coef, coded, *refs):
    arrived, rounded_ref, sent_refs, value_refs = refs[:5], refs[5], refs[6:10], refs[10:]
    fields = []
    for at in range(4):
        value = adjoint_value(at, index, coef, *arrived)
        if index + 2 == top:
            value = value - coef[top] * arrived[0][at].astype(f32)
        for ref in value_refs:
            ref[at] = value
        fields.append(value.astype(bf16))
        rounded_ref[at] = fields[-1]
    push(coded, fields, *sent_refs)


def block_gradients(slots, at, left, windows, listed, store):
    for k in range(listed):
        slot = slots[at * listed + k]
        right = jnp.concatenate([window[slot] for window in windows], axis=1)
        store(k, lax.dot_general(left, right, (((1,), (1,)), ((), ())), preferred_element_type=f32))


def middle_gradient_kernel(parts, slots, *refs):
    count = len(parts)
    adjoints, (sums_ref, windows) = refs[:count], refs[-2:]
    listed = sums_ref.shape[1]
    first = count
    for t in range(count):
        fill_window(refs[first : first + parts[t]], windows.at[t])
        first += parts[t]
    for at in range(4):
        left = [jnp.transpose(2.0 * a[at].astype(f32)).astype(bf16) for a in adjoints]

        def store(k, total, at=at):
            sums_ref[at, k] = total

        block_gradients(slots, at, jnp.concatenate(left, axis=1), [windows.at[t] for t in range(count)], listed, store)


def first_gradient_kernel(scale, slots, coef, older_ref, start_ref, before_ref, *refs):
    arrived, sums_ref = refs[:-1], refs[-1]
    listed = sums_ref.shape[1]
    for at in range(4):
        value = adjoint_value(at, 1, coef, *arrived) - older_ref[at]

        def store(k, total, at=at):
            sums_ref[at, k] = (before_ref[at, k] + total) * scale

        block_gradients(slots, at, jnp.transpose(value).astype(bf16), (start_ref,), listed, store)


def last_kernel(index, scale, rows, slots, coef, coded, *refs):
    before_ref, sums_ref, adjoint_ref, early_ref, density_hbm, grad_hbm, density, grad, window, density_sem, grad_sem = refs[4:]
    fill_window(refs[:4], window)
    listed = early_ref.shape[1]
    copies = []
    for at in range(4):
        place = (rows[at // 2], at % 2)
        value = 2.0 * window_product(at, coded, refs[:4]) - before_ref[at]
        density[at] = sums_ref[at] + coef[index] * value
        copies.append(pltpu.make_async_copy(density.at[at], density_hbm.at[place], density_sem.at[at]))
        copies[-1].start()

        def store(k, total, at=at):
            grad[at, k] = (early_ref[at, k] + total).astype(bf16)

        block_gradients(slots, at, adjoint_ref[at] * bf16(2.0 * scale), (window,), listed, store)
        copies.append(pltpu.make_async_copy(grad.at[at], grad_hbm.at[place], grad_sem.at[at]))
        copies[-1].start()
    for copy in copies:
        copy.wait()


def pair_shards(hamiltonian, neighbours, probe_seeds, coefficients, cotangent):
    rows_x, rows_y, listed, width = hamiltonian.shape[:4]
    probes = cotangent.shape[3]
    terms = coefficients.shape[0]
    top = terms - 1
    blocks = rows_x * rows_y
    span_x = rows_x * lax.axis_size("gx")
    span_y = rows_y * lax.axis_size("gy")
    vmem = pl.BlockSpec(memory_space=pltpu.VMEM)
    smem = pl.BlockSpec(memory_space=pltpu.SMEM)
    hbm = pl.BlockSpec(memory_space=pltpu.HBM)

    def field(count, dtype):
        return jax.ShapeDtypeStruct((count, width, probes), dtype)

    def turned(count, dtype):
        return jax.ShapeDtypeStruct((count, probes, width), dtype)

    apply_flops = 2 * blocks * listed * width * width * probes
    sent_shapes = [turned(4, bf16), turned(4, f32), turned(4, f32), turned(4, bf16)]
    window_scratch = pltpu.VMEM((16, width, probes), bf16)

    def kept(values):
        return tuple(pltpu.with_memory_space_constraint(value, pltpu.VMEM) for value in values)

    def call(name, kernel, scalars, operands, out_shape, scratch=(), flops=apply_flops, out_specs=None, in_specs=None):
        return pl.pallas_call(
            kernel,
            in_specs=[smem] * len(scalars) + (in_specs or [vmem] * len(operands)),
            out_specs=out_specs or [vmem] * len(out_shape),
            out_shape=out_shape,
            scratch_shapes=list(scratch),
            compiler_params=pltpu.CompilerParams(vmem_limit_bytes=VMEM_BYTES),
            cost_estimate=pl.CostEstimate(flops=flops, bytes_accessed=1024 * 1024, transcendentals=0),
            name=name,
        )(*scalars, *operands)

    gradient_sums = jax.ShapeDtypeStruct((blocks, listed, width, width), f32)
    shapes = [jax.ShapeDtypeStruct((2,), jnp.int32), jax.ShapeDtypeStruct((blocks * listed,), jnp.int32)]
    shapes += [jax.ShapeDtypeStruct((blocks, 9, width, width), bf16), field(16, bf16), field(4, f32)]
    shapes += [turned(4, bf16), field(4, bf16), field(4, bf16)] + sent_shapes
    rows, slots, coded, start, term, cot_t, adjoint, rounded, to_near, own, to_across, to_far = call(
        "first",
        functools.partial(first_kernel, top, span_x, span_y),
        (),
        tuple(
            pltpu.with_memory_space_constraint(value, pltpu.HBM)
            for value in (probe_seeds.reshape(1, probes), coefficients, neighbours, hamiltonian, cotangent)
        ),
        shapes,
        out_specs=[smem] * 2 + [vmem] * (len(shapes) - 2),
        scratch=(
            pltpu.VMEM((1, probes), jnp.int32),
            pltpu.SMEM(coefficients.shape, f32),
            pltpu.SMEM(neighbours.shape, jnp.int32),
            pltpu.VMEM((blocks, listed, width, width), bf16),
            pltpu.VMEM((blocks, width, probes), bf16),
            pltpu.SemaphoreType.DMA((3,)),
            pltpu.SemaphoreType.DMA((4,)),
            pltpu.SemaphoreType.DMA((4,)),
        ),
        flops=2 * apply_flops,
        in_specs=[hbm] * 5,
    )
    (coded,) = kept((coded,))
    adjoints = {top: adjoint}
    windows = []
    before, sums = start, term
    for index in range(2, terms):
        at = terms - index
        outer, inner = call(
            "pack_rows", pack_rows_kernel, (), kept((rounded, swap_y(rounded))), [field(4, bf16)] * 2, flops=0
        )
        near = swap_near(inner)
        window = kept((swap_far(outer), outer, inner, near))
        from_near, from_far = swap_near(to_near), swap_far(to_far)
        if index == top:
            middle = call(
                "middle_gradient",
                functools.partial(middle_gradient_kernel, (4,) * len(windows)),
                (slots,),
                kept(tuple(adjoints[t] for t in range(2, top)) + tuple(part for shown in windows for part in shown)),
                [gradient_sums],
                scratch=(pltpu.VMEM((terms - 3, 16, width, probes), bf16),),
                flops=(terms - 3) * apply_flops,
            )[0]
            from_near, middle = lax.optimization_barrier((from_near, middle))
        (to_across,) = call(
            "pack_across", pack_across_kernel, (), kept((to_across, from_near, from_far)), [turned(4, bf16)], flops=0
        )
        arrived = kept((cot_t, own, swap_y(to_across), from_near, from_far))
        if index == top:
            break
        windows.append(window)
        has_term = index + 2 <= top
        density, rounded, *following = call(
            "forward",
            functools.partial(forward_kernel, index, has_term),
            (coefficients,), (coded,) + window + kept((before, sums)),
            [field(4, f32), field(4, bf16)] + [field(4, f32)] * has_term,
        )
        before, sums = term, density
        term = following[0] if has_term else None
        has_value = at == 3
        adjoints[at], to_near, own, to_across, to_far, *rest = call(
            "adjoint",
            functools.partial(adjoint_kernel, at, top),
            (coefficients,), (coded,) + arrived,
            [turned(4, bf16)] + sent_shapes + [turned(4, f32)] * has_value,
        )
        if has_value:
            older = rest[0]
    early = call(
        "first_gradient",
        functools.partial(first_gradient_kernel, 1.0 / probes),
        (slots, coefficients), kept((older, start, middle)) + arrived,
        [gradient_sums],
    )[0]
    density, gradient = call(
        "last",
        functools.partial(last_kernel, top, 1.0 / probes),
        (rows, slots, coefficients), (coded,) + window + kept((before, sums, adjoints[top], early)),
        [
            jax.ShapeDtypeStruct(cotangent.shape, f32),
            jax.ShapeDtypeStruct(hamiltonian.shape, bf16),
        ],
        scratch=(
            pltpu.VMEM((4, width, probes), f32),
            pltpu.VMEM((blocks, listed, width, width), bf16),
            window_scratch,
            pltpu.SemaphoreType.DMA((4,)),
            pltpu.SemaphoreType.DMA((4,)),
        ),
        flops=2 * apply_flops,
        out_specs=[hbm, hbm],
    )
    return density, gradient


def shards(hamiltonian, neighbours, probe_seeds, coefficients, cotangent):
    paired = (
        hamiltonian.shape[:2] == (2, 2)
        and lax.axis_size("gy") == 2
        and lax.axis_size("gx") % 2 == 0
        and hamiltonian.shape[2] % 2 == 0
        and coefficients.shape[0] == 5
    )
    run = pair_shards if paired else any_shards
    return run(hamiltonian, neighbours, probe_seeds, coefficients, cotangent)


def solution(mesh):
    placed = (
        P("gx", "gy", None, None, None),
        P("gx", "gy", None),
        P(),
        P(),
        P("gx", "gy", None, None),
    )
    return jax.shard_map(
        shards,
        mesh=mesh,
        in_specs=placed,
        out_specs=(P("gx", "gy", None, None), P("gx", "gy", None, None, None)),
        check_vma=False,
    )
```
